32 devices in a mesh: graph: 8 (over y, x, core), mp: 4 (over z).
Axes of the slice: x: 2, y: 2, z: 4, core: 2. Of those that a mesh axis runs over, the one named last changes fastest.
Arguments:
- edge_feats: bfloat16 [16384, 512], P('graph', 'mp'), may hold values from -6 to 6
- edge_source: int32 [16384], P('graph'), may hold values from 0 to 16383, as said below
- edge_target: int32 [16384], P('graph'), may hold values from 0 to 16383, as said below
- edge_live: int32 [16384], P('graph'), may hold values from 0 to 1, as said below
- trip_partner: int32 [8, 16384], P(None, 'graph'), may hold values from 0 to 16383, as said below
- trip_mask: int32 [8, 16384], P(None, 'graph'), may hold values 0 or 1
- trip_basis: bfloat16 [16384, 128], P('graph'), may hold values from -6 to 6
- atom_feats: bfloat16 [16384, 512], P('graph', 'mp'), may hold values from -6 to 6
- w_msg: bfloat16 [512, 512], P(None, 'mp'), may hold values from -0.25 to 0.25
- w_down: bfloat16 [512, 64], replicated, may hold values from -0.25 to 0.25
- w_bil: bfloat16 [1024, 64], replicated, may hold values from -0.1875 to 0.1875
- w_up: bfloat16 [64, 512], P(None, 'mp'), may hold values from -0.75 to 0.75
- w_atom: bfloat16 [512, 512], P(None, 'mp'), may hold values from -0.25 to 0.25
- w_edge: bfloat16 [512, 512], P(None, 'mp'), may hold values from -0.25 to 0.25
Outputs:
- edge_out: bfloat16 [16384, 512], P('graph', 'mp')
- atom_out: bfloat16 [16384, 512], P('graph', 'mp')
The draws below stay inside these ranges and needn't reach their ends.
Inputs may be any that keep to these rules, and one draw needn't show every extreme that they name: `edge_target`: edge slots lie in blocks of 256: the slots of graph shard g for destination shard d are slots (g * 8 + d) * 256 onward; every source atom of shard g's slots lies in atoms g * 2048 to (g + 1) * 2048 - 1, every target atom of a block for d in shard d's atoms. `edge_source`: source atoms belong to the shard that holds the slot. `edge_live`: in each block of 256 slots the live slots come first, at least one; in every draw some destination shard gets all 256 slots live from every source shard. `trip_partner`: A partner edge is a slot of the same block of 256 slots as the edge.
All inputs are finite; a program needn't handle non-finite values. No bound on the sum of `trip_mask` on one device may be relied on, other than what follows from the above.
Results may differ from the reference program's by a relative error of at most 0.01.
Values may be sent and summed in bfloat16 or wider, within the bound.
No kernel may reach another device: no remote copies, remote signals or barrier semaphores. Data moves between devices by JAX's collectives and lax.ppermute only.
A program may use at most 192 MiB of HBM per device.

```python
import jax
import jax.numpy as jnp
from jax import lax

D = 512
DT = 64
NB = 16
SLOTS = 8
CAP = 256
ATOM_DEV = 2048
E_DEV = 2048
EDGES = 16384
ATOMS = 16384
N_GRAPH = 8


def bucket_counts(key):
    base = jax.random.randint(jax.random.fold_in(key, 11), (N_GRAPH, N_GRAPH), 1, CAP // 2 + 1)
    scores = jax.random.randint(jax.random.fold_in(key, 12), (N_GRAPH,), 0, 1 << 20)
    scores = scores * N_GRAPH + jnp.arange(N_GRAPH, dtype=jnp.int32)
    order = jnp.argsort(scores, stable=True)
    ranks = jnp.zeros((N_GRAPH,), jnp.int32).at[order].set(jnp.arange(N_GRAPH, dtype=jnp.int32))
    hot_dest = ranks < 3
    return jnp.where(hot_dest[None, :], CAP, base)


def slot_layout():
    position = jnp.arange(EDGES, dtype=jnp.int32)
    owner = position // (N_GRAPH * CAP)
    dest = position // CAP % N_GRAPH
    within = position % CAP
    return (owner, dest, within)


def draw_edge_live(key, part):
    counts = bucket_counts(key)
    owner, dest, within = slot_layout()
    return (within < counts[owner, dest]).astype(jnp.int32)


def draw_edge_target(key, part):
    owner, dest, within = slot_layout()
    local = jax.random.randint(jax.random.fold_in(key, 21), (EDGES,), 0, ATOM_DEV)
    return dest * ATOM_DEV + local


def draw_edge_source(key, part):
    owner, dest, within = slot_layout()
    local = jax.random.randint(jax.random.fold_in(key, 31), (EDGES,), 0, ATOM_DEV)
    return owner * ATOM_DEV + local


def draw_trip_partner(key, part):
    block_start = jnp.arange(EDGES, dtype=jnp.int32) // CAP * CAP
    local = jax.random.randint(jax.random.fold_in(key, 41), (SLOTS, EDGES), 0, CAP)
    return block_start[None, :] + local


def place_ends(values, stream_key, low, high):
    spot = [jax.random.randint(jax.random.fold_in(stream_key, axis), (), 0, length) for axis, length in enumerate(values.shape)]
    widest = values.shape.index(max(values.shape))
    next_to = spot[:widest] + [(spot[widest] + 1) % values.shape[widest]] + spot[widest + 1:]
    return values.at[tuple(spot)].set(low).at[tuple(next_to)].set(high)


def steps_of(rng, shape, shards, smallest, largest):
    gain = 1.0
    for dim, shards_of in shards:
        heights = jax.random.uniform(jax.random.fold_in(jax.random.fold_in(rng, 6), dim), (shards_of,), jnp.float32, smallest / len(shards), largest / len(shards))
        gain = gain * jnp.repeat(jnp.exp(heights), shape[dim] // shards_of).reshape((-1,) + (1,) * (len(shape) - 1 - dim))
    return gain


def normal_values(key, dims, deviation, most, split=(), held_as=jnp.bfloat16):
    factor_of = steps_of(key, dims, split, -0.22, 0.18) if split else 1.0
    values = jax.random.normal(key, dims, jnp.float32) * deviation * factor_of
    return jnp.minimum(jnp.maximum(values, -most), most).astype(held_as)


def setup_inputs(seed: int = 0) -> dict:
    arg_keys = jax.random.split(jax.random.key(seed), 15)
    edge_feats = normal_values(arg_keys[0], (EDGES, D), 1.0, 6.0, ((0, 8), (1, 4)))
    edge_source = draw_edge_source(jax.random.fold_in(arg_keys[14], 71), 0)
    edge_target = draw_edge_target(jax.random.fold_in(arg_keys[14], 71), 0)
    edge_live = draw_edge_live(jax.random.fold_in(arg_keys[14], 71), 0)
    trip_partner = draw_trip_partner(jax.random.fold_in(arg_keys[14], 71), 0)
    trip_mask = place_ends((jax.random.randint(arg_keys[5], (SLOTS, EDGES), 0, 4) < 3).astype(jnp.int32), jax.random.fold_in(arg_keys[5], 1), 0, 1)
    trip_basis = normal_values(arg_keys[6], (EDGES, SLOTS * NB), 1.0, 6.0, ((0, 8),))
    atom_feats = normal_values(arg_keys[7], (ATOMS, D), 1.0, 6.0, ((0, 8), (1, 4)))
    w_msg = normal_values(arg_keys[8], (D, D), D ** -0.5, 0.25, ((1, 4),))
    w_down = normal_values(arg_keys[9], (D, DT), D ** -0.5, 0.25)
    w_bil = normal_values(arg_keys[10], (NB * DT, DT), (NB * DT) ** -0.5, 0.1875)
    w_up = normal_values(arg_keys[11], (DT, D), DT ** -0.5, 0.75, ((1, 4),))
    w_atom = normal_values(arg_keys[12], (D, D), D ** -0.5, 0.25, ((1, 4),))
    w_edge = normal_values(arg_keys[13], (D, D), D ** -0.5, 0.25, ((1, 4),))
    return {"edge_feats": edge_feats, "edge_source": edge_source, "edge_target": edge_target, "edge_live": edge_live, "trip_partner": trip_partner, "trip_mask": trip_mask, "trip_basis": trip_basis, "atom_feats": atom_feats, "w_msg": w_msg, "w_down": w_down, "w_bil": w_bil, "w_up": w_up, "w_atom": w_atom, "w_edge": w_edge}


def reference(edge_feats, edge_source, edge_target, edge_live, trip_partner, trip_mask, trip_basis, atom_feats, w_msg, w_down, w_bil, w_up, w_atom, w_edge):
    hid = jnp.dot(edge_feats, w_msg, preferred_element_type=jnp.float32)
    message = edge_feats.astype(jnp.float32) + jax.nn.silu(hid)
    down = jnp.dot(edge_feats, w_down, preferred_element_type=jnp.float32).astype(jnp.bfloat16)
    blocks = EDGES // E_DEV

    def one_block(index):
        begin = (index * E_DEV).astype(jnp.int32)
        partner = lax.dynamic_slice_in_dim(trip_partner, begin, E_DEV, 1)
        masked = lax.dynamic_slice_in_dim(trip_mask, begin, E_DEV, 1)
        basis = lax.dynamic_slice_in_dim(trip_basis, begin, E_DEV, 0).reshape(E_DEV, SLOTS, NB)
        weights = basis.astype(jnp.float32) * jnp.transpose(masked).astype(jnp.float32)[:, :, None]
        picked = jnp.take(down, partner, axis=0).astype(jnp.float32)
        mixed = jnp.einsum('esb,sea->eba', weights, picked).astype(jnp.bfloat16)
        return jnp.dot(mixed.reshape(E_DEV, NB * DT), w_bil, preferred_element_type=jnp.float32).astype(jnp.bfloat16)

    bil = lax.map(one_block, jnp.arange(blocks, dtype=jnp.int32)).reshape(EDGES, DT)
    total = message + jnp.dot(bil, w_up, preferred_element_type=jnp.float32)
    outgoing = (total * edge_live.astype(jnp.float32)[:, None]).astype(jnp.bfloat16)
    agg = jax.ops.segment_sum(outgoing.astype(jnp.float32), edge_target, num_segments=ATOMS)
    atom_mid = (atom_feats.astype(jnp.float32) + agg).astype(jnp.bfloat16)
    ahid = jnp.dot(atom_mid, w_atom, preferred_element_type=jnp.float32)
    atom_out = (atom_mid.astype(jnp.float32) + jax.nn.silu(ahid)).astype(jnp.bfloat16)
    pair = (jnp.take(atom_out, edge_source, axis=0).astype(jnp.float32) * jnp.take(atom_out, edge_target, axis=0).astype(jnp.float32)).astype(jnp.bfloat16)
    ehid = jnp.dot(pair, w_edge, preferred_element_type=jnp.float32)
    edge_out = (total + jax.nn.silu(ehid)).astype(jnp.bfloat16)
    return edge_out, atom_out
```

```python
import functools

import jax
import jax.numpy as jnp
from jax import lax
from jax.experimental import pallas as pl
from jax.experimental.pallas import tpu as pltpu
from jax.sharding import PartitionSpec as P

NB = 16
SLOTS = 8
CAP = 256
BF = jnp.bfloat16
F32 = jnp.float32
VMEM_LIMIT = 40 * 1024 * 1024


def shard_at(plane, slot, n_graph, n_mp):
    half = n_mp // 2
    odd = (slot % 2) ^ (plane // half)
    chip = (slot // 2) * n_mp + (plane + half * odd) % n_mp
    return 2 * chip + odd


def silu(v):
    return v / (1.0 + jnp.exp(-v))


def dot(a, b):
    return jnp.dot(a, b, preferred_element_type=F32)


def dot_t(a, b):
    return lax.dot_general(a, b, (((1,), (1,)), ((), ())), preferred_element_type=F32)


def call(kernel, out_shapes, info, args, scratch=(), grid=(1,), in_specs=None, out_specs=None, flops=0, moved=0):
    whole = lambda s: pl.BlockSpec(s.shape, functools.partial(lambda n, *_: (0,) * n, len(s.shape)))
    in_specs = [whole(a) if in_specs is None or in_specs[i] is None else in_specs[i] for i, a in enumerate(args)]
    out_specs = [
        whole(o) if out_specs is None or out_specs[i] is None else out_specs[i] for i, o in enumerate(out_shapes)
    ]
    return pl.pallas_call(
        kernel,
        out_shape=list(out_shapes),
        grid_spec=pltpu.PrefetchScalarGridSpec(
            num_scalar_prefetch=1, grid=grid, in_specs=in_specs, out_specs=out_specs, scratch_shapes=list(scratch)
        ),
        compiler_params=pltpu.CompilerParams(vmem_limit_bytes=VMEM_LIMIT),
        cost_estimate=pl.CostEstimate(flops=flops, bytes_accessed=moved, transcendentals=0),
    )(info, *args)


def sds(shape, dtype=BF):
    return jax.ShapeDtypeStruct(tuple(shape), dtype)


def block_rows(i):
    return pl.ds(pl.multiple_of(i * CAP, CAP), CAP)


def lanes(i, width):
    return pl.ds(pl.multiple_of(i * width, width), width)


def column(row):
    wide = jnp.broadcast_to(row.astype(F32), (8, row.shape[1]))
    return jnp.transpose(wide)[:, :1].astype(jnp.int32)


def solution(mesh):
    G = mesh.shape["graph"]
    M = mesh.shape["mp"]
    per = G // M
    at = functools.partial(shard_at, n_graph=G, n_mp=M)
    both = ("graph", "mp")

    def over_mp(x, k):
        return lax.ppermute(x, "mp", [(i, i ^ k) for i in range(M)])

    def over_plane(x, k):
        return lax.ppermute(x, "graph", [(i, i ^ k) for i in range(G)])

    home_to_plane = [
        (at(z, s) * M + f, (s * M + f) * M + z) for z in range(M) for s in range(per) for f in range(M)
    ]
    plane_to_home = [(b, a) for a, b in home_to_plane]

    def source_route(r):
        return [
            ((s * M + f) * M + z, at(z, s) * M + (f ^ r)) for z in range(M) for s in range(per) for f in range(M)
        ]

    def prepare(info, ef, tgt, src, wm, wu, wa, we, *outs):
        g, m = info[0], info[1]
        chunks, (ids, w1, w2) = outs[:M], outs[M:]
        for k in range(M):
            for s in range(per):
                chunks[k][s * CAP : (s + 1) * CAP, :] = ef[block_rows(at(m ^ k, s)), :]
        core = g % 2
        half, uhalf = w1.shape[0] - wu.shape[0] // 2, wu.shape[0] // 2
        w1[:half, :] = wm[pl.ds(pl.multiple_of(core * half, half), half), :]
        w1[half:, :] = wu[pl.ds(pl.multiple_of(core * uhalf, uhalf), uhalf), :]
        w2[:half, :] = wa[pl.ds(pl.multiple_of(core * half, half), half), :]
        w2[half:, :] = we[pl.ds(pl.multiple_of(core * half, half), half), :]
        atoms = info[2]
        for d in range(G):
            ids[d, 0:1, :] = lax.rem(tgt[pl.ds(at(m, d // M), 1), :], atoms)
            ids[d, 1:, :] = lax.rem(src[...], atoms)

    def triplets(info, *refs):
        m = info[1]
        xs, (partner, mask, basis, wdt, wbt, x_out, bil_out, mixed) = refs[:M], refs[M:]
        w = xs[0].shape[1]
        for k in range(M):
            x_out[:, lanes(m ^ k, w)] = xs[k][...]
        downt = dot_t(wdt[...], x_out[...]).astype(BF)
        dt = downt.shape[0]
        ids = lax.rem(partner[...], CAP)
        rows = lax.broadcasted_iota(jnp.int32, (CAP, CAP), 0)
        picked = []
        for s in range(SLOTS):
            onehot = (rows == ids[s : s + 1, :]).astype(F32).astype(BF)
            picked.append(dot(downt, onehot))
        basist = jnp.transpose(basis[...].astype(F32))
        maskf = mask[...].astype(F32)
        weight = [basist[s * NB : (s + 1) * NB, :] * maskf[s : s + 1, :] for s in range(SLOTS)]
        for b in range(NB):
            acc = weight[0][b : b + 1, :] * picked[0]
            for s in range(1, SLOTS):
                acc = acc + weight[s][b : b + 1, :] * picked[s]
            mixed[b * dt : (b + 1) * dt, :] = acc.astype(BF)
        bilt = dot(wbt[...], mixed[...])
        bil_out[...] = jnp.transpose(bilt).astype(BF)

    def put_weights(m, mine, other, dst, core, half, upto, width):
        start = upto
        for k in range(M):
            cols = lanes(m ^ k, width)
            dst[pl.ds(pl.multiple_of(core * half, half), half), cols] = mine[k][start : start + half, :]
            dst[pl.ds(pl.multiple_of((1 - core) * half, half), half), cols] = other[k][start : start + half, :]

    def messages(info, *refs):
        g, m = info[0], info[1]
        mine, other = refs[:M], refs[M : 2 * M]
        x, bil, live, total_out, out, wm, wu = refs[2 * M :]
        width = out.shape[3]
        half = wm.shape[0] // 2

        @pl.when(pl.program_id(0) == 0)
        def _():
            put_weights(m, mine, other, wm, g % 2, half, 0, width)
            put_weights(m, mine, other, wu, g % 2, wu.shape[0] // 2, half, width)

        hid = dot(x[...], wm[...])
        total = x[...].astype(F32) + silu(hid) + dot(bil[...], wu[...])
        total_out[...] = total
        alive = column(live[pl.ds(at(m, pl.program_id(0)), 1), :]).astype(F32)
        sent = (total * alive).astype(BF)
        for f in range(M):
            out[0, f] = sent[:, f * width : (f + 1) * width]

    def aggregate(info, incoming, ids, af, *outs):
        f = info[0] % M
        part = outs[0].shape[0]
        for r in range(M):
            q = f ^ r
            rows = lax.broadcasted_iota(jnp.int32, (part, CAP), 0) + q * part

            def add(g, acc):
                onehot = (rows == ids[g, 0:1, :]).astype(F32).astype(BF)
                return acc + dot(onehot, incoming[g])

            acc = lax.fori_loop(0, G, add, jnp.zeros(outs[0].shape, F32), unroll=G <= 8)
            base = af[pl.ds(pl.multiple_of(q * part, part), part), :].astype(F32)
            outs[r][...] = (base + acc).astype(BF)

    def atom_layer(info, *refs):
        g, m = info[0], info[1]
        f = g % M
        xs, mine, other = refs[:M], refs[M : 2 * M], refs[2 * M : 3 * M]
        outs, (x, wa) = refs[3 * M : 4 * M], refs[4 * M :]
        width = xs[0].shape[1]
        for r in range(M):
            x[:, lanes(f ^ r, width)] = xs[r][...]
        put_weights(m, mine, other, wa, g % 2, wa.shape[0] // 2, 0, width)
        ahid = dot(x[...], wa[...])
        x[...] = (x[...].astype(F32) + silu(ahid)).astype(BF)
        for r in range(M):
            outs[r][...] = x[:, lanes(f ^ r, width)]

    def pick_rows(row, table):
        atoms = table.shape[0]
        onehot = lax.broadcasted_iota(jnp.int32, (CAP, atoms), 1) == column(row)
        return dot(onehot.astype(F32).astype(BF), table[...]).astype(BF)

    def sources(info, *refs):
        g, m = info[0], info[1]
        f, slot = g % M, g // M
        parts, ids, outs, table = refs[:M], refs[M], refs[M + 1 : 2 * M + 1], refs[2 * M + 1]
        part = parts[0].shape[0]
        for r in range(M):
            table[pl.ds(pl.multiple_of((f ^ r) * part, part), part), :] = parts[r][...]
        mine = at(m, slot)
        for r in range(M):
            for s in range(per):
                row = ids[mine, pl.ds(1 + at(f ^ r, s), 1), :]
                outs[r][s * CAP : (s + 1) * CAP, :] = pick_rows(row, table)

    def targets(info, table, ids, out):
        def one(g, _):
            out[g] = pick_rows(ids[g, 0:1, :], table)
            return 0

        lax.fori_loop(0, G, one, 0, unroll=G <= 8)

    def edges(info, *refs):
        g, m = info[0], info[1]
        srcs, mine, other = refs[:M], refs[M : 2 * M], refs[2 * M : 3 * M]
        tgt, total = refs[3 * M : 3 * M + 2]
        outs, (x, we) = refs[3 * M + 2 : 4 * M + 2], refs[4 * M + 2 :]
        width = srcs[0].shape[1]

        @pl.when(pl.program_id(0) == 0)
        def _():
            put_weights(m, mine, other, we, g % 2, we.shape[0] // 2, we.shape[0] // 2, width)

        for r in range(M):
            f = m ^ r
            x[:, lanes(f, width)] = (srcs[r][...].astype(F32) * tgt[0, f].astype(F32)).astype(BF)
        ehid = dot(x[...], we[...])
        x[...] = (total[...] + silu(ehid)).astype(BF)
        for k in range(M):
            outs[k][...] = x[:, lanes(m ^ k, width)]

    def assemble(info, *refs):
        m = info[1]
        parts, out = refs[:M], refs[M]
        for k in range(M):
            for s in range(per):
                out[block_rows(at(m ^ k, s)), :] = parts[k][s * CAP : (s + 1) * CAP, :]

    def local(ef, esrc, etgt, live, partner, mask, basis, af, w_msg, w_down, w_bil, w_up, w_atom, w_edge):
        rows, width = ef.shape
        atoms = af.shape[0]
        depth = w_msg.shape[0]
        dt = w_down.shape[1]
        chunk = per * CAP
        part = atoms // M
        g = lax.axis_index("graph")
        m = lax.axis_index("mp")
        info = jnp.stack([g, m, jnp.int32(atoms)]).astype(jnp.int32)
        w1_rows = depth // 2 + dt // 2
        *chunks, ids, w1, w2 = call(
            prepare,
            [sds((chunk, width))] * M + [sds((G, 1 + G, CAP), jnp.int32), sds((w1_rows, width)), sds((depth, width))],
            info,
            [ef, etgt.reshape(G, CAP), esrc.reshape(G, CAP), w_msg, w_up, w_atom, w_edge],
        )
        xs = [chunks[0]] + [over_mp(chunks[k], k) for k in range(1, M)]
        w1s = [w1] + [over_mp(w1, k) for k in range(1, M)]
        ids = lax.all_to_all(ids, "graph", split_axis=0, concat_axis=0, tiled=True)

        blk = lambda i, info: at(info[1], i)
        x, bil = call(
            triplets,
            [sds((chunk, depth)), sds((chunk, dt))],
            info,
            xs + [partner, mask, basis, w_down.T, w_bil.T],
            scratch=[pltpu.VMEM((NB * dt, CAP), BF)],
            grid=(per,),
            in_specs=[pl.BlockSpec((CAP, width), lambda i, info: (i, 0))] * M
            + [pl.BlockSpec((SLOTS, CAP), lambda i, info: (0, blk(i, info)))] * 2
            + [pl.BlockSpec((CAP, SLOTS * NB), lambda i, info: (blk(i, info), 0)), None, None],
            out_specs=[
                pl.BlockSpec((CAP, depth), lambda i, info: (i, 0)),
                pl.BlockSpec((CAP, dt), lambda i, info: (i, 0)),
            ],
        )
        w1o = [over_plane(w, 1) for w in w1s]
        total, outgoing = call(
            messages,
            [sds((chunk, depth), F32), sds((per, M, CAP, width))],
            info,
            w1s + w1o + [x, bil, live.reshape(G, CAP)],
            scratch=[pltpu.VMEM((depth, depth), BF), pltpu.VMEM((dt, depth), BF)],
            grid=(per,),
            in_specs=[None] * (2 * M)
            + [
                pl.BlockSpec((CAP, depth), lambda i, info: (i, 0)),
                pl.BlockSpec((CAP, dt), lambda i, info: (i, 0)),
                None,
            ],
            out_specs=[
                pl.BlockSpec((CAP, depth), lambda i, info: (i, 0)),
                pl.BlockSpec((1, M, CAP, width), lambda i, info: (i, 0, 0, 0)),
            ],
        )
        incoming = lax.all_to_all(outgoing.reshape(G, CAP, width), "graph", split_axis=0, concat_axis=0, tiled=True)
        af_later, w2_later, _ = lax.optimization_barrier((af, w2, xs[1]))
        af_plane = lax.ppermute(af_later, both, home_to_plane)
        w2s = [w2_later] + [over_mp(w2_later, k) for k in range(1, M)]
        w2o = [over_plane(w, 1) for w in w2s]

        mids = call(aggregate, [sds((part, width))] * M, info, [incoming, ids, af_plane])
        mids = [mids[0]] + [over_plane(mids[r], r) for r in range(1, M)]
        outs = call(
            atom_layer,
            [sds((part, width))] * M,
            info,
            mids + w2s + w2o,
            scratch=[pltpu.VMEM((part, depth), BF), pltpu.VMEM((depth, depth), BF)],
        )
        outs = [outs[0]] + [over_plane(outs[r], r) for r in range(1, M)]
        *srcs, table = call(sources, [sds((chunk, width))] * M + [sds((atoms, width))], info, list(outs) + [ids])
        srcs = [lax.ppermute(srcs[r], both, source_route(r)) for r in range(M)]
        (named,) = call(targets, [sds((G, CAP, width))], info, [table, ids])
        tgt = lax.all_to_all(named, "graph", split_axis=0, concat_axis=0, tiled=True)
        atom_out = lax.ppermute(table, both, plane_to_home)
        outs = call(
            edges,
            [sds((chunk, width))] * M,
            info,
            srcs + w2s + w2o + [tgt.reshape(per, M, CAP, width), total],
            scratch=[pltpu.VMEM((CAP, depth), BF), pltpu.VMEM((depth, depth), BF)],
            grid=(per,),
            in_specs=[pl.BlockSpec((CAP, width), lambda i, info: (i, 0))] * M
            + [None] * (2 * M)
            + [
                pl.BlockSpec((1, M, CAP, width), lambda i, info: (i, 0, 0, 0)),
                pl.BlockSpec((CAP, depth), lambda i, info: (i, 0)),
            ],
            out_specs=[pl.BlockSpec((CAP, width), lambda i, info: (i, 0))] * M,
        )
        outs = [outs[0]] + [over_mp(outs[k], k) for k in range(1, M)]
        (edge_out,) = call(assemble, [sds((rows, width))], info, list(outs))
        return (edge_out, atom_out)

    return jax.shard_map(
        local,
        mesh=mesh,
        in_specs=(
            P("graph", "mp"),
            P("graph"),
            P("graph"),
            P("graph"),
            P(None, "graph"),
            P(None, "graph"),
            P("graph", None),
            P("graph", "mp"),
            P(None, "mp"),
            P(),
            P(),
            P(None, "mp"),
            P(None, "mp"),
            P(None, "mp"),
        ),
        out_specs=(P("graph", "mp"), P("graph", "mp")),
        check_vma=False,
    )
```

```python
import functools

import jax
import jax.numpy as jnp
from jax import lax
from jax.experimental import pallas as pl
from jax.experimental.pallas import tpu as pltpu
from jax.sharding import PartitionSpec as P

NB = 16
SLOTS = 8
CAP = 256
LANES = 128
BF = jnp.bfloat16
F32 = jnp.float32
VMEM_LIMIT = 40 * 1024 * 1024


def shard_at(plane, slot, n_graph, n_mp):
    half = n_mp // 2
    odd = (slot % 2) ^ (plane // half)
    chip = (slot // 2) * n_mp + (plane + half * odd) % n_mp
    return 2 * chip + odd


def silu(v):
    return v / (1.0 + jnp.exp(-v))


def dot(a, b):
    return jnp.dot(a, b, preferred_element_type=F32)


def dot_t(a, b):
    return lax.dot_general(a, b, (((1,), (1,)), ((), ())), preferred_element_type=F32)


def call(kernel, out_shapes, info, args, scratch=(), grid=(1,), in_specs=None, out_specs=None, flops=0, moved=0):
    whole = lambda s: pl.BlockSpec(s.shape, functools.partial(lambda n, *_: (0,) * n, len(s.shape)))
    in_specs = [whole(a) if in_specs is None or in_specs[i] is None else in_specs[i] for i, a in enumerate(args)]
    out_specs = [
        whole(o) if out_specs is None or out_specs[i] is None else out_specs[i] for i, o in enumerate(out_shapes)
    ]
    return pl.pallas_call(
        kernel,
        out_shape=list(out_shapes),
        grid_spec=pltpu.PrefetchScalarGridSpec(
            num_scalar_prefetch=1, grid=grid, in_specs=in_specs, out_specs=out_specs, scratch_shapes=list(scratch)
        ),
        compiler_params=pltpu.CompilerParams(vmem_limit_bytes=VMEM_LIMIT),
        cost_estimate=pl.CostEstimate(flops=int(flops), bytes_accessed=moved, transcendentals=0),
    )(info, *args)


def sds(shape, dtype=BF):
    return jax.ShapeDtypeStruct(tuple(shape), dtype)


def block_rows(i):
    return pl.ds(pl.multiple_of(i * CAP, CAP), CAP)


def lanes(i, width):
    return pl.ds(pl.multiple_of(i * width, width), width)


def column(row):
    wide = jnp.broadcast_to(row.astype(F32), (8, row.shape[1]))
    return jnp.transpose(wide)[:, :1].astype(jnp.int32)


def solution(mesh):
    G = mesh.shape["graph"]
    M = mesh.shape["mp"]
    per = G // M
    at = functools.partial(shard_at, n_graph=G, n_mp=M)
    both = ("graph", "mp")

    def over_mp(x, k):
        return lax.ppermute(x, "mp", [(i, i ^ k) for i in range(M)])

    def over_plane(x, k):
        return lax.ppermute(x, "graph", [(i, i ^ k) for i in range(G)])

    home_to_plane = [
        (at(z, s) * M + f, (s * M + f) * M + z) for z in range(M) for s in range(per) for f in range(M)
    ]

    def source_route(r):
        return [
            ((s * M + f) * M + z, at(z, s) * M + (f ^ r)) for z in range(M) for s in range(per) for f in range(M)
        ]

    def split_rows(info, ef, *refs):
        m = info[1]
        outs, sem = refs[:M], refs[M]
        copies = []
        for k in range(M):
            for s in range(per):
                copies.append(
                    pltpu.make_async_copy(
                        ef.at[block_rows(at(m ^ k, s)), :],
                        outs[k].at[s * CAP : (s + 1) * CAP, :],
                        sem.at[k * per + s],
                    )
                )
        for c in copies:
            c.start()
        for c in copies:
            c.wait()

    def pack(info, tgt, src, wm, wu, ids, w1):
        g, m, atoms = info[0], info[1], info[2]
        core = g % 2
        uhalf = wu.shape[0] // 2
        half = w1.shape[0] - uhalf
        w1[:half, :] = wm[pl.ds(pl.multiple_of(core * half, half), half), :]
        w1[half:, :] = wu[pl.ds(pl.multiple_of(core * uhalf, uhalf), uhalf), :]
        for d in range(G):
            ids[d, 0:1, :] = lax.rem(tgt[pl.ds(at(m, d // M), 1), :], atoms)
            ids[d, 1:, :] = lax.rem(src[...], atoms)

    def pack_later(info, wa, we, w2):
        core = info[0] % 2
        half = w2.shape[0] // 2
        w2[:half, :] = wa[pl.ds(pl.multiple_of(core * half, half), half), :]
        w2[half:, :] = we[pl.ds(pl.multiple_of(core * half, half), half), :]

    def triplets(info, *refs):
        m = info[1]
        xs, (partner, mask, basis, wdt, wbt, x_out, bil_out, mixed) = refs[:M], refs[M:]
        w = xs[0].shape[1]
        for k in range(M):
            x_out[:, lanes(m ^ k, w)] = xs[k][...]
        downt = dot_t(wdt[...], x_out[...]).astype(BF)
        dt = downt.shape[0]
        ids = lax.rem(partner[...], CAP)
        rows = lax.broadcasted_iota(jnp.int32, (CAP, CAP), 0)
        picked = []
        for s in range(SLOTS):
            onehot = (rows == ids[s : s + 1, :]).astype(F32).astype(BF)
            picked.append(dot(downt, onehot))
        basist = jnp.transpose(basis[...].astype(F32))
        maskf = mask[...].astype(F32)
        weight = [basist[s * NB : (s + 1) * NB, :] * maskf[s : s + 1, :] for s in range(SLOTS)]
        for b in range(NB):
            acc = weight[0][b : b + 1, :] * picked[0]
            for s in range(1, SLOTS):
                acc = acc + weight[s][b : b + 1, :] * picked[s]
            mixed[b * dt : (b + 1) * dt, :] = acc.astype(BF)
        bilt = dot(wbt[...], mixed[...])
        bil_out[...] = jnp.transpose(bilt).astype(BF)

    def put_weights(m, mine, other, dst, core, half, upto, width):
        start = upto
        for k in range(M):
            cols = lanes(m ^ k, width)
            dst[pl.ds(pl.multiple_of(core * half, half), half), cols] = mine[k][start : start + half, :]
            dst[pl.ds(pl.multiple_of((1 - core) * half, half), half), cols] = other[k][start : start + half, :]

    def messages(info, *refs):
        g, m = info[0], info[1]
        mine, other = refs[:M], refs[M : 2 * M]
        x, bil, live, total_out, out, wm, wu = refs[2 * M :]
        width = out.shape[3]
        half = wm.shape[0] // 2

        @pl.when(pl.program_id(0) == 0)
        def _():
            put_weights(m, mine, other, wm, g % 2, half, 0, width)
            put_weights(m, mine, other, wu, g % 2, wu.shape[0] // 2, half, width)

        hid = dot(x[...], wm[...])
        total = x[...].astype(F32) + silu(hid) + dot(bil[...], wu[...])
        total_out[...] = total
        alive = column(live[pl.ds(at(m, pl.program_id(0)), 1), :]).astype(F32)
        sent = (total * alive).astype(BF)
        for f in range(M):
            out[0, f] = sent[:, f * width : (f + 1) * width]

    def aggregate(info, incoming, ids, af, *refs):
        f = info[0] % M
        outs, onehot = refs[:M], refs[M]
        part = outs[0].shape[0]
        low = lax.broadcasted_iota(jnp.int32, (LANES, CAP), 0)
        for r in range(M):
            q = f ^ r

            def fill(g, _):
                row = ids[g, 0:1, :]
                near = (low == lax.rem(row, LANES)).astype(F32).astype(BF)
                far = jnp.broadcast_to(lax.div(row, LANES) - q * (part // LANES), (LANES, CAP)).astype(F32).astype(BF)
                for h in range(part // LANES):
                    onehot[h * LANES : (h + 1) * LANES, lanes(g, CAP)] = jnp.where(
                        far == BF(h), near, jnp.zeros_like(near)
                    )
                return 0

            lax.fori_loop(0, G, fill, 0, unroll=G <= 8)
            acc = dot(onehot[...], incoming[...])
            base = af[pl.ds(pl.multiple_of(q * part, part), part), :].astype(F32)
            outs[r][...] = (base + acc).astype(BF)

    def atom_layer(info, *refs):
        g, m = info[0], info[1]
        f = g % M
        xs, mine, other = refs[:M], refs[M : 2 * M], refs[2 * M : 3 * M]
        outs, (x, wa) = refs[3 * M : 4 * M], refs[4 * M :]
        width = xs[0].shape[1]
        for r in range(M):
            x[:, lanes(f ^ r, width)] = xs[r][...]
        put_weights(m, mine, other, wa, g % 2, wa.shape[0] // 2, 0, width)
        ahid = dot(x[...], wa[...])
        x[...] = (x[...].astype(F32) + silu(ahid)).astype(BF)
        for r in range(M):
            outs[r][...] = x[:, lanes(f ^ r, width)]

    def pick_rows(row, table, onehot):
        col = column(row)
        near = (lax.broadcasted_iota(jnp.int32, (CAP, LANES), 1) == lax.rem(col, LANES)).astype(F32).astype(BF)
        far = jnp.broadcast_to(lax.div(col, LANES), (CAP, LANES)).astype(F32).astype(BF)
        for h in range(table.shape[0] // LANES):
            onehot[:, h * LANES : (h + 1) * LANES] = jnp.where(far == BF(h), near, jnp.zeros_like(near))
        return dot(onehot[...], table[...]).astype(BF)

    def sources(info, *refs):
        g, m = info[0], info[1]
        f, slot = g % M, g // M
        parts, ids, outs, table, onehot = refs[:M], refs[M], refs[M + 1 : 2 * M + 1], refs[2 * M + 1], refs[2 * M + 2]
        part = parts[0].shape[0]
        for r in range(M):
            table[pl.ds(pl.multiple_of((f ^ r) * part, part), part), :] = parts[r][...]
        mine = at(m, slot)
        for r in range(M):
            for s in range(per):
                row = ids[mine, pl.ds(1 + at(f ^ r, s), 1), :]
                outs[r][s * CAP : (s + 1) * CAP, :] = pick_rows(row, table, onehot.at[s % 2])

    def targets(info, table, ids, out, onehot):
        def one(g, _):
            out[g] = pick_rows(ids[g, 0:1, :], table, onehot.at[g % 2])
            return 0

        lax.fori_loop(0, G, one, 0, unroll=G <= 8)

    def edges(info, *refs):
        g, m = info[0], info[1]
        srcs, mine, other = refs[:M], refs[M : 2 * M], refs[2 * M : 3 * M]
        tgt, total = refs[3 * M : 3 * M + 2]
        outs, (x, we) = refs[3 * M + 2 : 4 * M + 2], refs[4 * M + 2 :]
        width = srcs[0].shape[1]

        @pl.when(pl.program_id(0) == 0)
        def _():
            put_weights(m, mine, other, we, g % 2, we.shape[0] // 2, we.shape[0] // 2, width)

        for r in range(M):
            f = m ^ r
            x[:, lanes(f, width)] = (srcs[r][...].astype(F32) * tgt[0, f].astype(F32)).astype(BF)
        ehid = dot(x[...], we[...])
        x[...] = (total[...] + silu(ehid)).astype(BF)
        for k in range(M):
            outs[k][...] = x[:, lanes(m ^ k, width)]

    def assemble(info, *refs):
        m = info[1]
        parts, out = refs[:M], refs[M]
        for k in range(M):
            for s in range(per):
                out[block_rows(at(m ^ k, s)), :] = parts[k][s * CAP : (s + 1) * CAP, :]

    def assemble_atoms(info, *refs):
        m = info[1]
        parts, out = refs[:M], refs[M]
        part = parts[0].shape[0]
        for r in range(M):
            out[pl.ds(pl.multiple_of((m ^ r) * part, part), part), :] = parts[r][...]

    def local(ef, esrc, etgt, live, partner, mask, basis, af, w_msg, w_down, w_bil, w_up, w_atom, w_edge):
        rows, width = ef.shape
        atoms = af.shape[0]
        depth = w_msg.shape[0]
        dt = w_down.shape[1]
        chunk = per * CAP
        part = atoms // M
        g = lax.axis_index("graph")
        m = lax.axis_index("mp")
        info = jnp.stack([g, m, jnp.int32(atoms)]).astype(jnp.int32)
        w1_rows = depth // 2 + dt // 2
        chunks = call(
            split_rows,
            [sds((chunk, width))] * M,
            info,
            [ef],
            scratch=[pltpu.SemaphoreType.DMA((M * per,))],
            in_specs=[pl.BlockSpec(memory_space=pl.ANY)],
        )
        ids, w1 = call(
            pack,
            [sds((G, 1 + G, CAP), jnp.int32), sds((w1_rows, width))],
            info,
            [etgt.reshape(G, CAP), esrc.reshape(G, CAP), w_msg, w_up],
            flops=1.0e9,
        )
        xs = [chunks[0]] + [over_mp(chunks[k], k) for k in range(1, M)]
        w1s = [w1] + [over_mp(w1, k) for k in range(1, M)]
        ids = lax.all_to_all(ids, "graph", split_axis=0, concat_axis=0, tiled=True)
        basis, ids = lax.optimization_barrier((basis, ids))

        blk = lambda i, info: at(info[1], i)
        x, bil = call(
            triplets,
            [sds((chunk, depth)), sds((chunk, dt))],
            info,
            xs + [partner, mask, basis, w_down.T, w_bil.T],
            scratch=[pltpu.VMEM((NB * dt, CAP), BF)],
            grid=(per,),
            in_specs=[pl.BlockSpec((CAP, width), lambda i, info: (i, 0))] * M
            + [pl.BlockSpec((SLOTS, CAP), lambda i, info: (0, blk(i, info)))] * 2
            + [pl.BlockSpec((CAP, SLOTS * NB), lambda i, info: (blk(i, info), 0)), None, None],
            out_specs=[
                pl.BlockSpec((CAP, depth), lambda i, info: (i, 0)),
                pl.BlockSpec((CAP, dt), lambda i, info: (i, 0)),
            ],
        )
        w1o = [over_plane(w, 1) for w in w1s]
        total, outgoing = call(
            messages,
            [sds((chunk, depth), F32), sds((per, M, CAP, width))],
            info,
            w1s + w1o + [x, bil, live.reshape(G, CAP)],
            scratch=[pltpu.VMEM((depth, depth), BF), pltpu.VMEM((dt, depth), BF)],
            grid=(per,),
            in_specs=[None] * (2 * M)
            + [
                pl.BlockSpec((CAP, depth), lambda i, info: (i, 0)),
                pl.BlockSpec((CAP, dt), lambda i, info: (i, 0)),
                None,
            ],
            out_specs=[
                pl.BlockSpec((CAP, depth), lambda i, info: (i, 0)),
                pl.BlockSpec((1, M, CAP, width), lambda i, info: (i, 0, 0, 0)),
            ],
        )
        incoming = lax.all_to_all(outgoing.reshape(G, CAP, width), "graph", split_axis=0, concat_axis=0, tiled=True)
        af_later, wa_later, we_later, _ = lax.optimization_barrier((af, w_atom, w_edge, xs[1]))
        af_plane = lax.ppermute(af_later, both, home_to_plane)
        (w2,) = call(pack_later, [sds((depth, width))], info, [wa_later, we_later], flops=1.0e9)
        w2s = [w2] + [over_mp(w2, k) for k in range(1, M)]

        mids = call(
            aggregate,
            [sds((part, width))] * M,
            info,
            [incoming.reshape(G * CAP, width), ids, af_plane],
            scratch=[pltpu.VMEM((part, G * CAP), BF)],
            flops=3.0e9,
        )
        *w2s, mid0 = lax.optimization_barrier((*w2s, mids[0]))
        w2o = [over_plane(w, 1) for w in w2s]
        mids = [mid0] + [over_plane(mids[r], r) for r in range(1, M)]
        outs = call(
            atom_layer,
            [sds((part, width))] * M,
            info,
            mids + w2s + w2o,
            scratch=[pltpu.VMEM((part, depth), BF), pltpu.VMEM((depth, depth), BF)],
            flops=1.5e9,
        )
        homeward = [lax.ppermute(outs[r], both, source_route(r)) for r in range(M)]
        outs = [outs[0]] + [over_plane(outs[r], r) for r in range(1, M)]
        *srcs, table = call(
            sources,
            [sds((chunk, width))] * M + [sds((atoms, width))],
            info,
            list(outs) + [ids],
            scratch=[pltpu.VMEM((2, CAP, atoms), BF)],
            flops=4.0e9,
        )
        srcs = [lax.ppermute(srcs[r], both, source_route(r)) for r in range(M)]
        (named,) = call(
            targets,
            [sds((G, CAP, width))],
            info,
            [table, ids],
            scratch=[pltpu.VMEM((2, CAP, atoms), BF)],
            flops=4.0e9,
        )
        tgt = lax.all_to_all(named, "graph", split_axis=0, concat_axis=0, tiled=True)
        outs = call(
            edges,
            [sds((chunk, width))] * M,
            info,
            srcs + w2s + w2o + [tgt.reshape(per, M, CAP, width), total],
            scratch=[pltpu.VMEM((CAP, depth), BF), pltpu.VMEM((depth, depth), BF)],
            grid=(per,),
            in_specs=[pl.BlockSpec((CAP, width), lambda i, info: (i, 0))] * M
            + [None] * (2 * M)
            + [
                pl.BlockSpec((1, M, CAP, width), lambda i, info: (i, 0, 0, 0)),
                pl.BlockSpec((CAP, depth), lambda i, info: (i, 0)),
            ],
            out_specs=[pl.BlockSpec((CAP, width), lambda i, info: (i, 0))] * M,
        )
        outs = [outs[0]] + [over_mp(outs[k], k) for k in range(1, M)]
        (atom_out,) = call(assemble_atoms, [sds((atoms, width))], info, homeward, flops=1.0e9)
        (edge_out,) = call(assemble, [sds((rows, width))], info, list(outs), flops=1.0e9)
        return (edge_out, atom_out)

    return jax.shard_map(
        local,
        mesh=mesh,
        in_specs=(
            P("graph", "mp"),
            P("graph"),
            P("graph"),
            P("graph"),
            P(None, "graph"),
            P(None, "graph"),
            P("graph", None),
            P("graph", "mp"),
            P(None, "mp"),
            P(),
            P(),
            P(None, "mp"),
            P(None, "mp"),
            P(None, "mp"),
        ),
        out_specs=(P("graph", "mp"), P("graph", "mp")),
        check_vma=False,
    )
```

```python
import functools

import jax
import jax.numpy as jnp
from jax import lax
from jax.experimental import pallas as pl
from jax.experimental.pallas import tpu as pltpu
from jax.sharding import PartitionSpec as P

NB = 16
SLOTS = 8
CAP = 256
LANES = 128
DIGIT = 64
ID_ROWS = 16
BF = jnp.bfloat16
F32 = jnp.float32
VMEM_LIMIT = 40 * 1024 * 1024


def silu(v):
    return v / (1.0 + jnp.exp(-v))


def dot(a, b):
    return jnp.dot(a, b, preferred_element_type=F32)


def dot_t(a, b):
    return lax.dot_general(a, b, (((1,), (1,)), ((), ())), preferred_element_type=F32)


def call(kernel, out_shapes, info, args, scratch=(), grid=(1,), in_specs=None, out_specs=None, flops=0, moved=0, vmem=VMEM_LIMIT):
    whole = lambda s: pl.BlockSpec(s.shape, functools.partial(lambda n, *_: (0,) * n, len(s.shape)))
    in_specs = [whole(a) if in_specs is None or in_specs[i] is None else in_specs[i] for i, a in enumerate(args)]
    out_specs = [
        whole(o) if out_specs is None or out_specs[i] is None else out_specs[i] for i, o in enumerate(out_shapes)
    ]
    return pl.pallas_call(
        kernel,
        out_shape=list(out_shapes),
        grid_spec=pltpu.PrefetchScalarGridSpec(
            num_scalar_prefetch=1, grid=grid, in_specs=in_specs, out_specs=out_specs, scratch_shapes=list(scratch)
        ),
        compiler_params=pltpu.CompilerParams(vmem_limit_bytes=vmem),
        cost_estimate=pl.CostEstimate(flops=int(flops), bytes_accessed=moved, transcendentals=0),
    )(info, *args)


def sds(shape, dtype=BF):
    return jax.ShapeDtypeStruct(tuple(shape), dtype)


def block_rows(i):
    return pl.ds(pl.multiple_of(i * CAP, CAP), CAP)


def lanes(i, width):
    return pl.ds(pl.multiple_of(i * width, width), width)


def column(row):
    wide = jnp.broadcast_to(row.astype(F32), (8, row.shape[1]))
    return jnp.transpose(wide)[:, :1].astype(jnp.int32)


def solution(mesh):
    G = mesh.shape["graph"]
    M = mesh.shape["mp"]
    per = G // M
    both = ("graph", "mp")

    def over_mp(x, k):
        return lax.ppermute(x, "mp", [(i, i ^ k) for i in range(M)])

    def over_plane(x, k):
        return lax.ppermute(x, "graph", [(i, i ^ k) for i in range(G)])

    def at(plane, slot):
        return slot * M + plane

    devices = [(s, i, z) for s in range(per) for i in range(M) for z in range(M)]

    def home(x, r):
        return lax.ppermute(x, both, [(at(i, s) * M + z, at(z, s) * M + (i ^ r)) for s, i, z in devices])

    def away(x, r):
        return lax.ppermute(x, both, [(at(j, s) * M + m, at(m ^ r, s) * M + j) for s, j, m in devices])

    def split(info, ef, wm, wa, we, wu, *refs):
        g, m = info[0], info[1]
        outs, share, sem = refs[:M], refs[M], refs[M + 1]
        moves = []
        for k in range(M):
            for s in range(per):
                moves.append((ef.at[block_rows(at(m ^ k, s)), :], outs[k].at[s * CAP : (s + 1) * CAP, :]))
        start = 0
        for w in (wm, wa, we):
            n = w.shape[0] // G
            moves.append((w.at[pl.ds(pl.multiple_of(g * n, n), n), :], share.at[start : start + n, :]))
            start += n
        moves.append((wu, share.at[start:, :]))
        copies = [pltpu.make_async_copy(src, dst, sem.at[i]) for i, (src, dst) in enumerate(moves)]
        for c in copies:
            c.start()
        for c in copies:
            c.wait()

    def stack(info, *refs):
        parts, outs = refs[:M], refs[M:]
        n = outs[0].shape[1]
        for j, out in enumerate(outs):
            for k in range(M):
                out[k] = parts[k][j * n : (j + 1) * n, :]

    def digits(ids):
        high = lax.div(ids, DIGIT)
        return high.astype(F32), (ids - high * DIGIT).astype(F32)

    def quarters(info, af, src, *outs):
        m, atoms = info[1], info[2]
        part = outs[1].shape[0]
        for r in range(M):
            outs[r][:part, :] = af[pl.ds(pl.multiple_of((m ^ r) * part, part), part), :]
        high, low = digits(lax.rem(src[...], atoms))
        lines = [x[:, c : c + LANES] for x in (high, low) for c in range(0, CAP, LANES)]
        outs[0][part:, :] = jnp.concatenate(lines, axis=0).astype(BF)

    def triplets(info, *refs):
        m = info[1]
        xs, (partner, mask, basis, wdt, wbt, x_out, bil_out, mixed) = refs[:M], refs[M:]
        w = xs[0].shape[1]
        for k in range(M):
            x_out[:, lanes(m ^ k, w)] = xs[k][...]
        downt = dot_t(wdt[...], x_out[...]).astype(BF)
        dt = downt.shape[0]
        ids = lax.rem(partner[...], CAP)
        rows = lax.broadcasted_iota(jnp.int32, (CAP, CAP), 0)
        picked = []
        for s in range(SLOTS):
            onehot = (rows == ids[s : s + 1, :]).astype(F32).astype(BF)
            picked.append(dot(downt, onehot))
        basist = jnp.transpose(basis[...].astype(F32))
        maskf = mask[...].astype(F32)
        weight = [basist[s * NB : (s + 1) * NB, :] * maskf[s : s + 1, :] for s in range(SLOTS)]
        for b in range(NB):
            acc = weight[0][b : b + 1, :] * picked[0]
            for s in range(1, SLOTS):
                acc = acc + weight[s][b : b + 1, :] * picked[s]
            mixed[b * dt : (b + 1) * dt, :] = acc.astype(BF)
        bilt = dot(wbt[...], mixed[...])
        bil_out[...] = jnp.transpose(bilt).astype(BF)

    def put_weights(m, shares, dst):
        n, width = shares.shape[1] // M, shares.shape[2]

        def put(g, _):
            for k in range(M):
                dst[pl.ds(pl.multiple_of(g * n, n), n), lanes(m ^ k, width)] = shares[g, k * n : (k + 1) * n, :]
            return 0

        lax.fori_loop(0, G, put, 0, unroll=G <= 8)

    def messages(info, *refs):
        m, atoms = info[1], info[2]
        up, (shares, ride, x, bil, live, tgt, total_out, out, wm, wu) = refs[:M], refs[M:]
        width = out.shape[3]
        first = out.shape[2] - CAP - ID_ROWS
        dt = wu.shape[0]

        @pl.when(pl.program_id(0) == 0)
        def _():
            put_weights(m, shares, wm)
            for k in range(M):
                wu[:, lanes(m ^ k, width)] = up[k][up[k].shape[0] - dt :, :]

        hid = dot(x[...], wm[...])
        total = x[...].astype(F32) + silu(hid) + dot(bil[...], wu[...])
        total_out[...] = total
        block = pl.ds(at(m, pl.program_id(0)), 1)
        sent = (total * column(live[block, :]).astype(F32)).astype(BF)
        lines = [x[:, c : c + LANES] for x in digits(lax.rem(tgt[block, :], atoms)) for c in range(0, CAP, LANES)]
        lines.append(jnp.zeros((ID_ROWS - len(lines), LANES), F32))
        lines = jnp.concatenate(lines, axis=0).astype(BF)
        for f in range(M):
            for j in range(M // 2):
                out[0, f, j * ride.shape[1] : (j + 1) * ride.shape[1], :] = ride[f % 2 * (M // 2) + j]
            out[0, f, first : first + CAP, :] = sent[:, f * width : (f + 1) * width]
            out[0, f, first + CAP :, :] = lines

    def aggregate(info, incoming, *refs):
        f = info[0] % M
        outs, (ids, ride, onehot, values, agg) = refs[:M], refs[M:]
        part, width = outs[0].shape
        half = agg.shape[0] // 2
        step = onehot.shape[0]
        first = incoming.shape[1] - CAP - ID_ROWS
        low = lax.broadcasted_iota(jnp.int32, (LANES, CAP), 0)

        def place(g, _):
            lines = incoming[g, first + CAP :, :].astype(F32)
            n = CAP // LANES
            high = jnp.concatenate([lines[c : c + 1, :] for c in range(n)], axis=1)
            row = high * DIGIT + jnp.concatenate([lines[n + c : n + c + 1, :] for c in range(n)], axis=1)
            ids[g] = row.astype(jnp.int32)
            ride[g] = incoming[g, :first, :]
            upper = (column(row) >= half).astype(F32)
            rows = incoming[g, first : first + CAP, :].astype(F32)
            values[block_rows(g), :width] = (rows * (1.0 - upper)).astype(BF)
            values[block_rows(g), width:] = (rows * upper).astype(BF)
            return 0

        lax.fori_loop(0, G, place, 0, unroll=G <= 8)
        for q in range(half // step):

            def fill(g, _):
                row = lax.rem(ids[g], half)
                near = (low == lax.rem(row, LANES)).astype(F32).astype(BF)
                far = jnp.broadcast_to(lax.div(row, LANES) - q * (step // LANES), (LANES, CAP)).astype(F32).astype(BF)
                for h in range(step // LANES):
                    onehot[h * LANES : (h + 1) * LANES, lanes(g, CAP)] = jnp.where(
                        far == BF(h), near, jnp.zeros_like(near)
                    )
                return 0

            lax.fori_loop(0, G, fill, 0, unroll=G <= 8)
            acc = dot(onehot[...], values[...]).astype(BF)
            agg[q * step : (q + 1) * step, :] = acc[:, :width]
            agg[half + q * step : half + (q + 1) * step, :] = acc[:, width:]
        for r in range(M):
            outs[r][...] = agg[pl.ds(pl.multiple_of((f ^ r) * part, part), part), :]

    def atom_layer(info, *refs):
        g, m = info[0], info[1]
        f = g % M
        sums, feats, halves = refs[:M], refs[M : 2 * M], refs[2 * M : 2 * M + 2]
        outs, (x, wa) = refs[2 * M + 2 : 3 * M + 2], refs[3 * M + 2 :]
        part, width = sums[0].shape
        for r in range(M):
            x[:, lanes(f ^ r, width)] = (feats[r][:part, :].astype(F32) + sums[r][...].astype(F32)).astype(BF)
        n = halves[0].shape[1] // (M // 2)

        def put(d, _):
            for core, half in ((g % 2, halves[0]), ((g + 1) % 2, halves[1])):
                for j in range(M // 2):
                    cols = lanes(m ^ (core * (M // 2) + j), width)
                    wa[pl.ds(pl.multiple_of(d * n, n), n), cols] = half[d, j * n : (j + 1) * n, :]
            return 0

        lax.fori_loop(0, G, put, 0, unroll=G <= 8)
        ahid = dot(x[...], wa[...])
        x[...] = (x[...].astype(F32) + silu(ahid)).astype(BF)
        for r in range(M):
            outs[r][...] = x[:, lanes(f ^ r, width)]

    def gather(info, *refs):
        f = info[0] % M
        parts, ids, sent, ride = refs[:M], refs[M], refs[M + 1], refs[M + 2]
        srcs, tgt, (table, onehot, src) = refs[M + 3 : 2 * M + 3], refs[2 * M + 3], refs[2 * M + 4 :]
        part, width = parts[0].shape
        half = table.shape[0]
        share = ride.shape[1]
        for r in range(M):
            q = f ^ r
            per_half = half // part
            rows = pl.ds(pl.multiple_of(lax.rem(q, per_half) * part, part), part)
            table[rows, lanes(lax.div(q, per_half), width)] = parts[r][...]

        def mark(row, line):
            col = column(row)
            upper = col >= half
            col = lax.rem(col, half)
            near = (lax.broadcasted_iota(jnp.int32, (CAP, LANES), 1) == lax.rem(col, LANES)).astype(F32).astype(BF)
            far = jnp.broadcast_to(lax.div(col, LANES), (CAP, LANES)).astype(F32).astype(BF)
            for h in range(half // LANES):
                onehot[line * CAP : (line + 1) * CAP, h * LANES : (h + 1) * LANES] = jnp.where(
                    far == BF(h), near, jnp.zeros_like(near)
                )
            return upper

        def pick(line, upper):
            found = dot(onehot[line * CAP : (line + 1) * CAP, :], table[...])
            return jnp.where(upper, found[:, width:], found[:, :width]).astype(BF)

        lines = sent[part:, :].astype(F32)
        n = CAP // LANES
        high = jnp.concatenate([lines[c * G : (c + 1) * G, :] for c in range(n)], axis=1)
        low = jnp.concatenate([lines[(n + c) * G : (n + c + 1) * G, :] for c in range(n)], axis=1)
        src[...] = (high * DIGIT + low).astype(jnp.int32)
        group = onehot.shape[0] // CAP
        places = [(r, s) for r in range(M) for s in range(per)]
        for start in range(0, G, group):
            now = places[start : start + group]
            upper = [mark(src[pl.ds(at(f ^ r, s), 1), :], j) for j, (r, s) in enumerate(now)]
            for j, (r, s) in enumerate(now):
                srcs[r][s * CAP : (s + 1) * CAP, :] = pick(j, upper[j])

        def several(b, _):
            upper = [mark(ids[b * group + j], j) for j in range(group)]
            for j in range(group):
                tgt[b * group + j, :CAP, :] = pick(j, upper[j])
                for k in range(M):
                    tgt[b * group + j, CAP + k * share : CAP + (k + 1) * share, :] = ride[k]
            return 0

        lax.fori_loop(0, G // group, several, 0, unroll=True)

    def edges(info, *refs):
        m = info[1]
        srcs, (shares, tgt, total) = refs[:M], refs[M : M + 3]
        outs, (x, we) = refs[M + 3 : 2 * M + 3], refs[2 * M + 3 :]
        width = srcs[0].shape[1]

        @pl.when(pl.program_id(0) == 0)
        def _():
            put_weights(m, shares, we)

        for r in range(M):
            f = m ^ r
            x[:, lanes(f, width)] = (srcs[r][...].astype(F32) * tgt[0, f].astype(F32)).astype(BF)
        ehid = dot(x[...], we[...])
        x[...] = (total[...] + silu(ehid)).astype(BF)
        for k in range(M):
            outs[k][...] = x[:, lanes(m ^ k, width)]

    def assemble(info, *refs):
        m = info[1]
        parts, out = refs[:M], refs[M]
        for k in range(M):
            for s in range(per):
                out[block_rows(at(m ^ k, s)), :] = parts[k][s * CAP : (s + 1) * CAP, :]

    def assemble_atoms(info, *refs):
        m = info[1]
        parts, out = refs[:M], refs[M]
        part = parts[0].shape[0]
        for r in range(M):
            out[pl.ds(pl.multiple_of((m ^ r) * part, part), part), :] = parts[r][...]

    def local(ef, esrc, etgt, live, partner, mask, basis, af, w_msg, w_down, w_bil, w_up, w_atom, w_edge):
        rows, width = ef.shape
        atoms = af.shape[0]
        depth = w_msg.shape[0]
        dt = w_down.shape[1]
        chunk = per * CAP
        part = atoms // M
        g = lax.axis_index("graph")
        m = lax.axis_index("mp")
        info = jnp.stack([g, m, jnp.int32(atoms)]).astype(jnp.int32)
        share = depth // G
        *chunks, w = call(
            split,
            [sds((chunk, width))] * M + [sds((3 * share + dt, width))],
            info,
            [ef, w_msg, w_atom, w_edge, w_up],
            scratch=[pltpu.SemaphoreType.DMA((M * per + 4,))],
            in_specs=[pl.BlockSpec(memory_space=pl.ANY)] * 5,
            vmem=60 * 1024 * 1024,
        )
        ws = [w] + [over_mp(w, k) for k in range(1, M)]
        xs = [chunks[0]] + [over_mp(chunks[k], k) for k in range(1, M)]
        feats = call(
            quarters,
            [sds((part + 2 * rows // LANES, width))] + [sds((part, width))] * (M - 1),
            info,
            [af, esrc.reshape(G, CAP)],
            flops=0.5e9,
        )
        wm, wa, we = call(stack, [sds((M, share, width))] * 3, info, ws)
        wm = lax.all_gather(wm, "graph", axis=0)

        blk = lambda i, info: at(info[1], i)
        x, bil = call(
            triplets,
            [sds((chunk, depth)), sds((chunk, dt))],
            info,
            xs + [partner, mask, basis, w_down.T, w_bil.T],
            scratch=[pltpu.VMEM((NB * dt, CAP), BF)],
            grid=(per,),
            in_specs=[pl.BlockSpec((CAP, width), lambda i, info: (i, 0))] * M
            + [pl.BlockSpec((SLOTS, CAP), lambda i, info: (0, blk(i, info)))] * 2
            + [pl.BlockSpec((CAP, SLOTS * NB), lambda i, info: (blk(i, info), 0)), None, None],
            out_specs=[
                pl.BlockSpec((CAP, depth), lambda i, info: (i, 0)),
                pl.BlockSpec((CAP, dt), lambda i, info: (i, 0)),
            ],
        )
        total, outgoing = call(
            messages,
            [sds((chunk, depth), F32), sds((per, M, M // 2 * share + CAP + ID_ROWS, width))],
            info,
            ws + [wm.reshape(G, M * share, width), wa, x, bil, live.reshape(G, CAP), etgt.reshape(G, CAP)],
            scratch=[pltpu.VMEM((depth, depth), BF), pltpu.VMEM((dt, depth), BF)],
            grid=(per,),
            in_specs=[None] * (M + 2)
            + [
                pl.BlockSpec((CAP, depth), lambda i, info: (i, 0)),
                pl.BlockSpec((CAP, dt), lambda i, info: (i, 0)),
                None,
                None,
            ],
            out_specs=[
                pl.BlockSpec((CAP, depth), lambda i, info: (i, 0)),
                pl.BlockSpec((1, M, M // 2 * share + CAP + ID_ROWS, width), lambda i, info: (i, 0, 0, 0)),
            ],
        )
        incoming = lax.all_to_all(
            outgoing.reshape(G, M // 2 * share + CAP + ID_ROWS, width), "graph", split_axis=0, concat_axis=0, tiled=True
        )
        *feats, _ = lax.optimization_barrier((*feats, outgoing))
        feats = [away(feats[r], r) for r in range(M)]
        *sums, ids, wa = call(
            aggregate,
            [sds((part, width))] * M + [sds((G, 1, CAP), jnp.int32), sds((G, M // 2 * share, width))],
            info,
            [incoming],
            scratch=[pltpu.VMEM((part, G * CAP), BF), pltpu.VMEM((G * CAP, 2 * width), BF), pltpu.VMEM((atoms, width), BF)],
            flops=3.0e9,
        )
        sums = [sums[0]] + [over_plane(sums[r], r) for r in range(1, M)]
        outs = call(
            atom_layer,
            [sds((part, width))] * M,
            info,
            sums + feats + [wa, over_plane(wa, 1)],
            scratch=[pltpu.VMEM((part, depth), BF), pltpu.VMEM((depth, depth), BF)],
            flops=1.5e9,
        )
        homeward = [home(outs[r], r) for r in range(M)]
        outs = [outs[0]] + [over_plane(outs[r], r) for r in range(1, M)]
        *srcs, named = call(
            gather,
            [sds((chunk, width))] * M + [sds((G, CAP + M * share, width))],
            info,
            outs + [ids, feats[0], we],
            scratch=[
                pltpu.VMEM((atoms // 2, 2 * width), BF),
                pltpu.VMEM((min(G, 8) * CAP, atoms // 2), BF),
                pltpu.VMEM((G, CAP), jnp.int32),
            ],
            flops=6.0e9,
        )
        srcs = [home(srcs[r], r) for r in range(M)]
        *homeward, named = lax.optimization_barrier((*homeward, named))
        tgt = lax.all_to_all(named, "graph", split_axis=0, concat_axis=0, tiled=True)
        outs = call(
            edges,
            [sds((chunk, width))] * M,
            info,
            srcs + [tgt, tgt.reshape(per, M, CAP + M * share, width), total],
            scratch=[pltpu.VMEM((CAP, depth), BF), pltpu.VMEM((depth, depth), BF)],
            grid=(per,),
            in_specs=[pl.BlockSpec((CAP, width), lambda i, info: (i, 0))] * M
            + [
                pl.BlockSpec((G, M * share, width), lambda i, info: (0, CAP // (M * share), 0)),
                pl.BlockSpec((1, M, CAP, width), lambda i, info: (i, 0, 0, 0)),
                pl.BlockSpec((CAP, depth), lambda i, info: (i, 0)),
            ],
            out_specs=[pl.BlockSpec((CAP, width), lambda i, info: (i, 0))] * M,
        )
        outs = [outs[0]] + [over_mp(outs[k], k) for k in range(1, M)]
        (atom_out,) = call(assemble_atoms, [sds((atoms, width))], info, homeward, flops=1.0e9)
        (edge_out,) = call(assemble, [sds((rows, width))], info, list(outs), flops=1.0e9)
        return (edge_out, atom_out)

    return jax.shard_map(
        local,
        mesh=mesh,
        in_specs=(
            P("graph", "mp"),
            P("graph"),
            P("graph"),
            P("graph"),
            P(None, "graph"),
            P(None, "graph"),
            P("graph", None),
            P("graph", "mp"),
            P(None, "mp"),
            P(),
            P(),
            P(None, "mp"),
            P(None, "mp"),
            P(None, "mp"),
        ),
        out_specs=(P("graph", "mp"), P("graph", "mp")),
        check_vma=False,
    )
```

```python
import functools

import jax
import jax.numpy as jnp
from jax import lax
from jax.experimental import pallas as pl
from jax.experimental.pallas import tpu as pltpu
from jax.sharding import PartitionSpec as P

NB = 16
SLOTS = 8
CAP = 256
LANES = 128
DIGIT = 64
ID_ROWS = 16
BF = jnp.bfloat16
F32 = jnp.float32
VMEM_LIMIT = 40 * 1024 * 1024


def silu(v):
    return v / (1.0 + jnp.exp(-v))


def dot(a, b):
    return jnp.dot(a, b, preferred_element_type=F32)


def dot_t(a, b):
    return lax.dot_general(a, b, (((1,), (1,)), ((), ())), preferred_element_type=F32)


def call(kernel, out_shapes, info, args, scratch=(), grid=(1,), in_specs=None, out_specs=None, flops=0, moved=0, vmem=VMEM_LIMIT):
    whole = lambda s: pl.BlockSpec(s.shape, functools.partial(lambda n, *_: (0,) * n, len(s.shape)))
    in_specs = [whole(a) if in_specs is None or in_specs[i] is None else in_specs[i] for i, a in enumerate(args)]
    out_specs = [
        whole(o) if out_specs is None or out_specs[i] is None else out_specs[i] for i, o in enumerate(out_shapes)
    ]
    return pl.pallas_call(
        kernel,
        out_shape=list(out_shapes),
        grid_spec=pltpu.PrefetchScalarGridSpec(
            num_scalar_prefetch=1, grid=grid, in_specs=in_specs, out_specs=out_specs, scratch_shapes=list(scratch)
        ),
        compiler_params=pltpu.CompilerParams(vmem_limit_bytes=vmem),
        cost_estimate=pl.CostEstimate(flops=int(flops), bytes_accessed=moved, transcendentals=0),
    )(info, *args)


def sds(shape, dtype=BF):
    return jax.ShapeDtypeStruct(tuple(shape), dtype)


def block_rows(i):
    return pl.ds(pl.multiple_of(i * CAP, CAP), CAP)


def lanes(i, width):
    return pl.ds(pl.multiple_of(i * width, width), width)


def column(row):
    wide = jnp.broadcast_to(row.astype(F32), (8, row.shape[1]))
    return jnp.transpose(wide)[:, :1].astype(jnp.int32)


def solution(mesh):
    G = mesh.shape["graph"]
    M = mesh.shape["mp"]
    per = G // M
    both = ("graph", "mp")

    def over_mp(x, k):
        return lax.ppermute(x, "mp", [(i, i ^ k) for i in range(M)])

    def over_plane(x, k):
        return lax.ppermute(x, "graph", [(i, i ^ k) for i in range(G)])

    def at(plane, slot):
        return slot * M + plane

    devices = [(s, i, z) for s in range(per) for i in range(M) for z in range(M)]

    def home(x, r):
        return lax.ppermute(x, both, [(at(i, s) * M + z, at(z, s) * M + (i ^ r)) for s, i, z in devices])

    def away(x, r):
        return lax.ppermute(x, both, [(at(j, s) * M + m, at(m ^ r, s) * M + j) for s, j, m in devices])

    def split(info, ef, wm, wa, we, wu, af, *refs):
        g, m = info[0], info[1]
        outs, share, quarters, sem = refs[:M], refs[M], refs[M + 1 : 2 * M + 1], refs[2 * M + 1]
        part = quarters[0].shape[0]
        moves = []
        for k in range(M):
            for s in range(per):
                moves.append((ef.at[block_rows(at(m ^ k, s)), :], outs[k].at[s * CAP : (s + 1) * CAP, :]))
        start = 0
        for w in (wm, wa, we):
            n = w.shape[0] // G
            moves.append((w.at[pl.ds(pl.multiple_of(g * n, n), n), :], share.at[start : start + n, :]))
            start += n
        moves.append((wu, share.at[start:, :]))
        for r in range(M):
            moves.append((af.at[pl.ds(pl.multiple_of((m ^ r) * part, part), part), :], quarters[r].at[:, :]))
        copies = [pltpu.make_async_copy(src, dst, sem.at[i]) for i, (src, dst) in enumerate(moves)]
        for c in copies:
            c.start()
        for c in copies:
            c.wait()

    def stack(info, *refs):
        parts, (out, we) = refs[:M], refs[M:]
        n = we.shape[1]
        for k in range(M):
            for j in range(out.shape[0] // (M * n)):
                out[(j * M + k) * n : (j * M + k + 1) * n, :] = parts[k][j * n : (j + 1) * n, :]
            we[k] = parts[k][2 * n : 3 * n, :]

    def digits(ids):
        high = lax.div(ids, DIGIT)
        return high.astype(F32), (ids - high * DIGIT).astype(F32)

    def triplets(info, *refs):
        m = info[1]
        xs, (partner, mask, basis, wdt, wbt, x_out, bil_out, mixed) = refs[:M], refs[M:]
        w = xs[0].shape[1]
        for k in range(M):
            x_out[:, lanes(m ^ k, w)] = xs[k][...]
        downt = dot_t(wdt[...], x_out[...]).astype(BF)
        dt = downt.shape[0]
        ids = lax.rem(partner[...], CAP)
        rows = lax.broadcasted_iota(jnp.int32, (CAP, CAP), 0)
        picked = []
        for s in range(SLOTS):
            onehot = (rows == ids[s : s + 1, :]).astype(F32).astype(BF)
            picked.append(dot(downt, onehot))
        basist = jnp.transpose(basis[...].astype(F32))
        maskf = mask[...].astype(F32)
        weight = [basist[s * NB : (s + 1) * NB, :] * maskf[s : s + 1, :] for s in range(SLOTS)]
        for b in range(NB):
            acc = weight[0][b : b + 1, :] * picked[0]
            for s in range(1, SLOTS):
                acc = acc + weight[s][b : b + 1, :] * picked[s]
            mixed[b * dt : (b + 1) * dt, :] = acc.astype(BF)
        bilt = dot(wbt[...], mixed[...])
        bil_out[...] = jnp.transpose(bilt).astype(BF)

    def put_weights(m, shares, dst):
        n, width = shares.shape[1] // M, shares.shape[2]

        def put(g, _):
            for k in range(M):
                dst[pl.ds(pl.multiple_of(g * n, n), n), lanes(m ^ k, width)] = shares[g, k * n : (k + 1) * n, :]
            return 0

        lax.fori_loop(0, G, put, 0, unroll=G <= 8)

    def put_shares(info, shares, dst):
        g, m = info[0], info[1]
        n, width = shares[0].shape[0] // M, shares[0].shape[1]
        for d in range(G):
            for k in range(M):
                here = pl.ds(pl.multiple_of((g ^ d) * n, n), n)
                dst[here, lanes(m ^ k, width)] = shares[d][k * n : (k + 1) * n, :]

    def messages(info, *refs):
        m, atoms = info[1], info[2]
        up, shares, (x, bil, live, tgt, src, total_out, out, wm, wu) = refs[:M], refs[M : M + G], refs[M + G :]
        width = out.shape[3]
        dt = wu.shape[0]

        @pl.when(pl.program_id(0) == 0)
        def _():
            put_shares(info, shares, wm)
            for k in range(M):
                wu[:, lanes(m ^ k, width)] = up[k][up[k].shape[0] - dt :, :]

        hid = dot(x[...], wm[...])
        total = x[...].astype(F32) + silu(hid) + dot(bil[...], wu[...])
        total_out[...] = total
        block = pl.ds(at(m, pl.program_id(0)), 1)
        sent = (total * column(live[block, :]).astype(F32)).astype(BF)
        ends = [digits(lax.rem(ids, atoms)) for ids in (tgt[block, :], src[...])]
        lines = [[x[:, c : c + LANES] for x in pair for c in range(0, CAP, LANES)] for pair in ends]
        lines[0].append(jnp.zeros((ID_ROWS - len(lines[0]), LANES), F32))
        lines = [jnp.concatenate(part, axis=0).astype(BF) for part in lines]
        for f in range(M):
            out[0, f, :CAP, :] = sent[:, f * width : (f + 1) * width]
            out[0, f, CAP : CAP + ID_ROWS, :] = lines[0]
            out[0, f, CAP + ID_ROWS :, :] = lines[1]

    def arrived(info, *refs):
        refs[-1][...] = jnp.zeros(refs[-1].shape, F32)

    def aggregate(info, incoming, _, *refs):
        f = info[0] % M
        outs, (ids, sent, onehot, values, agg) = refs[:M], refs[M:]
        part, width = outs[0].shape
        half = agg.shape[0] // 2
        step = onehot.shape[0]
        low = lax.broadcasted_iota(jnp.int32, (LANES, CAP), 0)

        def place(g, _):
            lines = incoming[g, CAP : CAP + ID_ROWS, :].astype(F32)
            n = CAP // LANES
            high = jnp.concatenate([lines[c : c + 1, :] for c in range(n)], axis=1)
            row = high * DIGIT + jnp.concatenate([lines[n + c : n + c + 1, :] for c in range(n)], axis=1)
            ids[g] = row.astype(jnp.int32)
            upper = (column(row) >= half).astype(F32)
            rows = incoming[g, :CAP, :].astype(F32)
            values[block_rows(g), :width] = (rows * (1.0 - upper)).astype(BF)
            values[block_rows(g), width:] = (rows * upper).astype(BF)
            return 0

        lax.fori_loop(0, G, place, 0, unroll=G <= 8)
        sent[...] = incoming[at(info[1], info[0] // M), CAP + ID_ROWS :, :]
        for q in range(half // step):

            def fill(g, _):
                row = lax.rem(ids[g], half)
                near = (low == lax.rem(row, LANES)).astype(F32).astype(BF)
                far = jnp.broadcast_to(lax.div(row, LANES) - q * (step // LANES), (LANES, CAP)).astype(F32).astype(BF)
                for h in range(step // LANES):
                    onehot[h * LANES : (h + 1) * LANES, lanes(g, CAP)] = jnp.where(
                        far == BF(h), near, jnp.zeros_like(near)
                    )
                return 0

            lax.fori_loop(0, G, fill, 0, unroll=G <= 8)
            acc = dot(onehot[...], values[...]).astype(BF)
            agg[q * step : (q + 1) * step, :] = acc[:, :width]
            agg[half + q * step : half + (q + 1) * step, :] = acc[:, width:]
        for r in range(M):
            outs[r][...] = agg[pl.ds(pl.multiple_of((f ^ r) * part, part), part), :]

    def atom_layer(info, *refs):
        g, m = info[0], info[1]
        f = g % M
        sums, feats, shares = refs[:M], refs[M : 2 * M], refs[2 * M : 2 * M + G]
        outs, (x, wa) = refs[2 * M + G : 3 * M + G], refs[3 * M + G :]
        part, width = sums[0].shape
        for r in range(M):
            x[:, lanes(f ^ r, width)] = (feats[r][...].astype(F32) + sums[r][...].astype(F32)).astype(BF)
        put_shares(info, shares, wa)
        ahid = dot(x[...], wa[...])
        x[...] = (x[...].astype(F32) + silu(ahid)).astype(BF)
        for r in range(M):
            outs[r][...] = x[:, lanes(f ^ r, width)]

    def gather(info, *refs):
        f = info[0] % M
        parts, ids, sent, ride = refs[:M], refs[M], refs[M + 1], refs[M + 2]
        srcs, tgt, (table, onehot, src) = refs[M + 3 : 2 * M + 3], refs[2 * M + 3], refs[2 * M + 4 :]
        part, width = parts[0].shape
        half = table.shape[0]
        share = ride.shape[1]
        for r in range(M):
            q = f ^ r
            per_half = half // part
            rows = pl.ds(pl.multiple_of(lax.rem(q, per_half) * part, part), part)
            table[rows, lanes(lax.div(q, per_half), width)] = parts[r][...]

        def mark(row, line):
            col = column(row)
            upper = col >= half
            col = lax.rem(col, half)
            near = (lax.broadcasted_iota(jnp.int32, (CAP, LANES), 1) == lax.rem(col, LANES)).astype(F32).astype(BF)
            far = jnp.broadcast_to(lax.div(col, LANES), (CAP, LANES)).astype(F32).astype(BF)
            for h in range(half // LANES):
                onehot[line * CAP : (line + 1) * CAP, h * LANES : (h + 1) * LANES] = jnp.where(
                    far == BF(h), near, jnp.zeros_like(near)
                )
            return upper

        def pick(line, upper):
            found = dot(onehot[line * CAP : (line + 1) * CAP, :], table[...])
            return jnp.where(upper, found[:, width:], found[:, :width]).astype(BF)

        lines = sent[...].astype(F32)
        n = CAP // LANES
        high = jnp.concatenate([lines[c * G : (c + 1) * G, :] for c in range(n)], axis=1)
        low = jnp.concatenate([lines[(n + c) * G : (n + c + 1) * G, :] for c in range(n)], axis=1)
        src[...] = (high * DIGIT + low).astype(jnp.int32)
        group = onehot.shape[0] // CAP
        places = [(r, s) for r in range(M) for s in range(per)]
        for start in range(0, G, group):
            now = places[start : start + group]
            upper = [mark(src[pl.ds(at(f ^ r, s), 1), :], j) for j, (r, s) in enumerate(now)]
            for j, (r, s) in enumerate(now):
                srcs[r][s * CAP : (s + 1) * CAP, :] = pick(j, upper[j])

        def several(b, _):
            upper = [mark(ids[b * group + j], j) for j in range(group)]
            for j in range(group):
                tgt[b * group + j, :CAP, :] = pick(j, upper[j])
                for k in range(M):
                    tgt[b * group + j, CAP + k * share : CAP + (k + 1) * share, :] = ride[k]
            return 0

        lax.fori_loop(0, G // group, several, 0, unroll=True)

    def edges(info, *refs):
        m = info[1]
        srcs, (shares, tgt, total) = refs[:M], refs[M : M + 3]
        outs, (x, we) = refs[M + 3 : 2 * M + 3], refs[2 * M + 3 :]
        width = srcs[0].shape[1]

        @pl.when(pl.program_id(0) == 0)
        def _():
            put_weights(m, shares, we)

        for r in range(M):
            f = m ^ r
            x[:, lanes(f, width)] = (srcs[r][...].astype(F32) * tgt[0, f].astype(F32)).astype(BF)
        ehid = dot(x[...], we[...])
        x[...] = (total[...] + silu(ehid)).astype(BF)
        for k in range(M):
            outs[k][...] = x[:, lanes(m ^ k, width)]

    def assemble(info, *refs):
        m = info[1]
        parts, out = refs[:M], refs[M]
        for k in range(M):
            for s in range(per):
                out[block_rows(at(m ^ k, s)), :] = parts[k][s * CAP : (s + 1) * CAP, :]

    def assemble_atoms(info, *refs):
        m = info[1]
        parts, out = refs[:M], refs[M]
        part = parts[0].shape[0]
        for r in range(M):
            out[pl.ds(pl.multiple_of((m ^ r) * part, part), part), :] = parts[r][...]

    def local(ef, esrc, etgt, live, partner, mask, basis, af, w_msg, w_down, w_bil, w_up, w_atom, w_edge):
        rows, width = ef.shape
        atoms = af.shape[0]
        depth = w_msg.shape[0]
        dt = w_down.shape[1]
        chunk = per * CAP
        id_rows = ID_ROWS + 2 * rows // LANES
        part = atoms // M
        g = lax.axis_index("graph")
        m = lax.axis_index("mp")
        info = jnp.stack([g, m, jnp.int32(atoms)]).astype(jnp.int32)
        share = depth // G
        first = call(
            split,
            [sds((chunk, width))] * M + [sds((3 * share + dt, width))] + [sds((part, width))] * M,
            info,
            [ef, w_msg, w_atom, w_edge, w_up, af],
            scratch=[pltpu.SemaphoreType.DMA((M * per + M + 4,))],
            in_specs=[pl.BlockSpec(memory_space=pl.ANY)] * 6,
            vmem=60 * 1024 * 1024,
        )
        chunks, w, feats = first[:M], first[M], first[M + 1 :]
        ws = [w] + [over_mp(w, k) for k in range(1, M)]
        xs = [chunks[0]] + [over_mp(chunks[k], k) for k in range(1, M)]
        wm, we = call(stack, [sds((2 * M * share, width)), sds((M, share, width))], info, ws, flops=3e10)
        even = [wm] + [over_plane(wm, x) for x in range(2, G, 2)]
        odd = [over_plane(w, 1) for w in even]
        wm = [w for pair in zip(even, odd) for w in pair]
        share_spec = lambda j: [pl.BlockSpec((M * share, width), lambda i, info: (j, 0))] * G

        blk = lambda i, info: at(info[1], i)
        x, bil = call(
            triplets,
            [sds((chunk, depth)), sds((chunk, dt))],
            info,
            xs + [partner, mask, basis, w_down.T, w_bil.T],
            scratch=[pltpu.VMEM((NB * dt, CAP), BF)],
            grid=(per,),
            in_specs=[pl.BlockSpec((CAP, width), lambda i, info: (i, 0))] * M
            + [pl.BlockSpec((SLOTS, CAP), lambda i, info: (0, blk(i, info)))] * 2
            + [pl.BlockSpec((CAP, SLOTS * NB), lambda i, info: (blk(i, info), 0)), None, None],
            out_specs=[
                pl.BlockSpec((CAP, depth), lambda i, info: (i, 0)),
                pl.BlockSpec((CAP, dt), lambda i, info: (i, 0)),
            ],
        )
        total, outgoing = call(
            messages,
            [sds((chunk, depth), F32), sds((per, M, CAP + id_rows, width))],
            info,
            ws + wm + [x, bil, live.reshape(G, CAP), etgt.reshape(G, CAP), esrc.reshape(G, CAP)],
            scratch=[pltpu.VMEM((depth, depth), BF), pltpu.VMEM((dt, depth), BF)],
            grid=(per,),
            in_specs=[None] * M + share_spec(0)
            + [
                pl.BlockSpec((CAP, depth), lambda i, info: (i, 0)),
                pl.BlockSpec((CAP, dt), lambda i, info: (i, 0)),
                None,
                None,
                None,
            ],
            out_specs=[
                pl.BlockSpec((CAP, depth), lambda i, info: (i, 0)),
                pl.BlockSpec((1, M, CAP + id_rows, width), lambda i, info: (i, 0, 0, 0)),
            ],
        )
        incoming = lax.all_to_all(
            outgoing.reshape(G, CAP + id_rows, width), "graph", split_axis=0, concat_axis=0, tiled=True
        )
        feats = [away(feats[r], r) for r in range(M)]
        (token,) = call(
            arrived,
            [sds((8, LANES), F32)],
            info,
            feats,
            in_specs=[pl.BlockSpec(memory_space=pl.ANY)] * M,
            flops=3e10,
        )
        *sums, ids, sent = call(
            aggregate,
            [sds((part, width))] * M + [sds((G, 1, CAP), jnp.int32), sds((2 * rows // LANES, width))],
            info,
            [incoming, token],
            scratch=[pltpu.VMEM((part, G * CAP), BF), pltpu.VMEM((G * CAP, 2 * width), BF), pltpu.VMEM((atoms, width), BF)],
            flops=3.0e9,
        )
        sums = [sums[0]] + [over_plane(sums[r], r) for r in range(1, M)]
        outs = call(
            atom_layer,
            [sds((part, width))] * M,
            info,
            sums + feats + wm,
            scratch=[pltpu.VMEM((part, depth), BF), pltpu.VMEM((depth, depth), BF)],
            in_specs=[None] * (2 * M) + share_spec(1),
            flops=1.5e9,
        )
        homeward = [home(outs[r], r) for r in range(M)]
        outs = [outs[0]] + [over_plane(outs[r], r) for r in range(1, M)]
        *srcs, named = call(
            gather,
            [sds((chunk, width))] * M + [sds((G, CAP + M * share, width))],
            info,
            outs + [ids, sent, we],
            scratch=[
                pltpu.VMEM((atoms // 2, 2 * width), BF),
                pltpu.VMEM((min(G, 8) * CAP, atoms // 2), BF),
                pltpu.VMEM((G, CAP), jnp.int32),
            ],
            flops=6.0e9,
        )
        srcs = [home(srcs[r], r) for r in range(M)]
        *homeward, named = lax.optimization_barrier((*homeward, named))
        tgt = lax.all_to_all(named, "graph", split_axis=0, concat_axis=0, tiled=True)
        outs = call(
            edges,
            [sds((chunk, width))] * M,
            info,
            srcs + [tgt, tgt.reshape(per, M, CAP + M * share, width), total],
            scratch=[pltpu.VMEM((CAP, depth), BF), pltpu.VMEM((depth, depth), BF)],
            grid=(per,),
            in_specs=[pl.BlockSpec((CAP, width), lambda i, info: (i, 0))] * M
            + [
                pl.BlockSpec((G, M * share, width), lambda i, info: (0, CAP // (M * share), 0)),
                pl.BlockSpec((1, M, CAP, width), lambda i, info: (i, 0, 0, 0)),
                pl.BlockSpec((CAP, depth), lambda i, info: (i, 0)),
            ],
            out_specs=[pl.BlockSpec((CAP, width), lambda i, info: (i, 0))] * M,
        )
        outs = [outs[0]] + [over_mp(outs[k], k) for k in range(1, M)]
        (atom_out,) = call(assemble_atoms, [sds((atoms, width))], info, homeward, flops=1.0e9)
        (edge_out,) = call(assemble, [sds((rows, width))], info, list(outs), flops=1.0e9)
        return (edge_out, atom_out)

    return jax.shard_map(
        local,
        mesh=mesh,
        in_specs=(
            P("graph", "mp"),
            P("graph"),
            P("graph"),
            P("graph"),
            P(None, "graph"),
            P(None, "graph"),
            P("graph", None),
            P("graph", "mp"),
            P(None, "mp"),
            P(),
            P(),
            P(None, "mp"),
            P(None, "mp"),
            P(None, "mp"),
        ),
        out_specs=(P("graph", "mp"), P("graph", "mp")),
        check_vma=False,
    )
```

```python
import functools

import jax
import jax.numpy as jnp
from jax import lax
from jax.experimental import pallas as pl
from jax.experimental.pallas import tpu as pltpu
from jax.sharding import PartitionSpec as P

NB = 16
SLOTS = 8
CAP = 256
LANES = 128
LANE_BITS = 7
DIGIT = 64
DIGIT_BITS = 6
ID_ROWS = 16
BF = jnp.bfloat16
F32 = jnp.float32
VMEM_LIMIT = 40 * 1024 * 1024


def silu(v):
    return v / (1.0 + jnp.exp(-v))


def dot(a, b):
    return jnp.dot(a, b, preferred_element_type=F32)


def dot_t(a, b):
    return lax.dot_general(a, b, (((1,), (1,)), ((), ())), preferred_element_type=F32)


def call(kernel, out_shapes, info, args, scratch=(), grid=(1,), in_specs=None, out_specs=None, flops=0, moved=0, vmem=VMEM_LIMIT):
    whole = lambda s: pl.BlockSpec(s.shape, functools.partial(lambda n, *_: (0,) * n, len(s.shape)))
    in_specs = [whole(a) if in_specs is None or in_specs[i] is None else in_specs[i] for i, a in enumerate(args)]
    out_specs = [
        whole(o) if out_specs is None or out_specs[i] is None else out_specs[i] for i, o in enumerate(out_shapes)
    ]
    return pl.pallas_call(
        kernel,
        out_shape=list(out_shapes),
        grid_spec=pltpu.PrefetchScalarGridSpec(
            num_scalar_prefetch=1, grid=grid, in_specs=in_specs, out_specs=out_specs, scratch_shapes=list(scratch)
        ),
        compiler_params=pltpu.CompilerParams(vmem_limit_bytes=vmem),
        cost_estimate=pl.CostEstimate(flops=int(flops), bytes_accessed=moved, transcendentals=0),
    )(info, *args)


def sds(shape, dtype=BF):
    return jax.ShapeDtypeStruct(tuple(shape), dtype)


def block_rows(i):
    return pl.ds(pl.multiple_of(i * CAP, CAP), CAP)


def lanes(i, width):
    return pl.ds(pl.multiple_of(i * width, width), width)


def column(row):
    wide = jnp.broadcast_to(row.astype(F32), (8, row.shape[1]))
    return jnp.transpose(wide)[:, :1].astype(jnp.int32)


def solution(mesh):
    G = mesh.shape["graph"]
    M = mesh.shape["mp"]
    per = G // M
    both = ("graph", "mp")

    def over_mp(x, k):
        return lax.ppermute(x, "mp", [(i, i ^ k) for i in range(M)])

    def over_plane(x, k):
        return lax.ppermute(x, "graph", [(i, i ^ k) for i in range(G)])

    def at(plane, slot):
        return slot * M + plane

    devices = [(s, i, z) for s in range(per) for i in range(M) for z in range(M)]

    def home(x, r):
        return lax.ppermute(x, both, [(at(i, s) * M + z, at(z, s) * M + (i ^ r)) for s, i, z in devices])

    def away(x, r):
        return lax.ppermute(x, both, [(at(j, s) * M + m, at(m ^ r, s) * M + j) for s, j, m in devices])

    def split(info, ef, wm, wa, we, wu, af, *refs):
        g, m = lax.axis_index("graph"), lax.axis_index("mp")
        outs, share, quarters, sem = refs[:M], refs[M], refs[M + 1 : 2 * M + 1], refs[2 * M + 1]
        part = quarters[0].shape[0]
        moves = []
        for k in range(M):
            for s in range(per):
                moves.append((ef.at[block_rows(at(m ^ k, s)), :], outs[k].at[s * CAP : (s + 1) * CAP, :]))
        start = 0
        for w in (wm, wa, we):
            n = w.shape[0] // G
            moves.append((w.at[pl.ds(pl.multiple_of(g * n, n), n), :], share.at[start : start + n, :]))
            start += n
        moves.append((wu, share.at[start:, :]))
        for r in range(M):
            moves.append((af.at[pl.ds(pl.multiple_of((m ^ r) * part, part), part), :], quarters[r].at[:, :]))
        copies = [pltpu.make_async_copy(src, dst, sem.at[i]) for i, (src, dst) in enumerate(moves)]
        for c in copies:
            c.start()
        for c in copies:
            c.wait()

    def stack(info, *refs):
        parts, (wm, wa, we) = refs[:M], refs[M:]
        n = we.shape[1]
        for k in range(M):
            wm[k * n : (k + 1) * n, :] = parts[k][:n, :]
            wa[k] = parts[k][n : 2 * n, :]
            we[k] = parts[k][2 * n : 3 * n, :]

    def digits(ids):
        return (ids >> DIGIT_BITS).astype(F32), (ids & (DIGIT - 1)).astype(F32)

    def triplets(info, *refs):
        m = info[1]
        xs, (partner, mask, basis, wdt, wbt, x_out, bil_out, mixed) = refs[:M], refs[M:]
        w = xs[0].shape[1]
        for k in range(M):
            x_out[:, lanes(m ^ k, w)] = xs[k][...]
        downt = dot_t(wdt[...], x_out[...]).astype(BF)
        dt = downt.shape[0]
        ids = partner[...] & (CAP - 1)
        rows = lax.broadcasted_iota(jnp.int32, (CAP, CAP), 0)
        picked = []
        for s in range(SLOTS):
            onehot = (rows == ids[s : s + 1, :]).astype(F32).astype(BF)
            picked.append(dot(downt, onehot))
        basist = jnp.transpose(basis[...].astype(F32))
        maskf = mask[...].astype(F32)
        weight = [basist[s * NB : (s + 1) * NB, :] * maskf[s : s + 1, :] for s in range(SLOTS)]
        for b in range(NB):
            acc = weight[0][b : b + 1, :] * picked[0]
            for s in range(1, SLOTS):
                acc = acc + weight[s][b : b + 1, :] * picked[s]
            mixed[b * dt : (b + 1) * dt, :] = acc.astype(BF)
        bilt = dot(wbt[...], mixed[...])
        bil_out[...] = jnp.transpose(bilt).astype(BF)

    def put_weights(m, shares, dst):
        n, width = shares.shape[1] // M, shares.shape[2]

        def put(g, _):
            for k in range(M):
                dst[pl.ds(pl.multiple_of(g * n, n), n), lanes(m ^ k, width)] = shares[g, k * n : (k + 1) * n, :]
            return 0

        lax.fori_loop(0, G, put, 0, unroll=G <= 8)

    def put_shares(info, shares, dst):
        g, m = info[0], info[1]
        n, width = shares[0].shape[0] // M, shares[0].shape[1]
        for d in range(G):
            for k in range(M):
                here = pl.ds(pl.multiple_of((g ^ d) * n, n), n)
                dst[here, lanes(m ^ k, width)] = shares[d][k * n : (k + 1) * n, :]

    def whole_weight(info, own, other, wa):
        g, m = info[0], info[1]
        n, width = own.shape[1] // (M // 2), own.shape[2]

        def put(d, _):
            for core, half in ((g % 2, own), ((g + 1) % 2, other)):
                for j in range(M // 2):
                    cols = lanes(m ^ (core * (M // 2) + j), width)
                    wa[pl.ds(pl.multiple_of(d * n, n), n), cols] = half[d, j * n : (j + 1) * n, :]
            return 0

        lax.fori_loop(0, G, put, 0, unroll=G <= 8)

    def messages(info, *refs):
        m, atoms = info[1], info[2]
        up, shares, (ride, x, bil, live, tgt, src, total_out, out, wm, wu) = refs[:M], refs[M : M + G], refs[M + G :]
        width = out.shape[3]
        dt = wu.shape[0]

        @pl.when(pl.program_id(0) == 0)
        def _():
            put_shares(info, shares, wm)
            for k in range(M):
                wu[:, lanes(m ^ k, width)] = up[k][up[k].shape[0] - dt :, :]

        hid = dot(x[...], wm[...])
        total = x[...].astype(F32) + silu(hid) + dot(bil[...], wu[...])
        total_out[...] = total
        block = pl.ds(at(m, pl.program_id(0)), 1)
        sent = (total * column(live[block, :]).astype(F32)).astype(BF)
        ends = [digits(lax.rem(ids, atoms)) for ids in (tgt[block, :], src[...])]
        lines = [[x[:, c : c + LANES] for x in pair for c in range(0, CAP, LANES)] for pair in ends]
        lines[0].append(jnp.zeros((ID_ROWS - len(lines[0]), LANES), F32))
        lines = [jnp.concatenate(part, axis=0).astype(BF) for part in lines]
        id_rows = CAP + ID_ROWS + lines[1].shape[0]
        for f in range(M):
            out[0, f, :CAP, :] = sent[:, f * width : (f + 1) * width]
            out[0, f, CAP : CAP + ID_ROWS, :] = lines[0]
            out[0, f, CAP + ID_ROWS : id_rows, :] = lines[1]
            for j in range(M // 2):
                here = slice(id_rows + j * ride.shape[1], id_rows + (j + 1) * ride.shape[1])
                out[0, f, here, :] = ride[f % 2 * (M // 2) + j]

    def arrived(info, *refs):
        refs[-1][...] = jnp.zeros(refs[-1].shape, F32)

    def aggregate(info, incoming, _, *refs):
        f = info[0] % M
        outs, (ids, sent, ride, onehot, values, agg) = refs[:M], refs[M:]
        part, width = outs[0].shape
        half = agg.shape[0] // 2
        step = onehot.shape[0]
        low = lax.broadcasted_iota(jnp.int32, (LANES, CAP), 0)

        def place(g, _):
            lines = incoming[g, CAP : CAP + ID_ROWS, :].astype(F32)
            n = CAP // LANES
            high = jnp.concatenate([lines[c : c + 1, :] for c in range(n)], axis=1)
            row = high * DIGIT + jnp.concatenate([lines[n + c : n + c + 1, :] for c in range(n)], axis=1)
            ids[g] = row.astype(jnp.int32)
            ride[g] = incoming[g, incoming.shape[1] - ride.shape[1] :, :]
            upper = (column(row) >= half).astype(F32)
            rows = incoming[g, :CAP, :].astype(F32)
            values[block_rows(g), :width] = (rows * (1.0 - upper)).astype(BF)
            values[block_rows(g), width:] = (rows * upper).astype(BF)
            return 0

        lax.fori_loop(0, G, place, 0, unroll=G <= 8)
        n = CAP + ID_ROWS
        sent[...] = incoming[at(info[1], info[0] // M), n : n + sent.shape[0], :]
        for q in range(half // step):

            def fill(g, _):
                row = ids[g]
                row = jnp.where(row >= half, row - half, row)
                near = (low == (row & (LANES - 1))).astype(F32).astype(BF)
                far = jnp.broadcast_to(((row >> LANE_BITS) - q * (step // LANES)).astype(F32), (LANES, CAP)).astype(BF)
                for h in range(step // LANES):
                    onehot[h * LANES : (h + 1) * LANES, lanes(g, CAP)] = jnp.where(
                        far == BF(h), near, jnp.zeros_like(near)
                    )
                return 0

            lax.fori_loop(0, G, fill, 0, unroll=G <= 8)
            acc = dot(onehot[...], values[...]).astype(BF)
            agg[q * step : (q + 1) * step, :] = acc[:, :width]
            agg[half + q * step : half + (q + 1) * step, :] = acc[:, width:]
        for r in range(M):
            outs[r][...] = agg[pl.ds(pl.multiple_of((f ^ r) * part, part), part), :]

    def atom_layer(info, *refs):
        g, m = info[0], info[1]
        f = g % M
        sums, feats, wa = refs[:M], refs[M : 2 * M], refs[2 * M]
        outs, x = refs[2 * M + 1 : 3 * M + 1], refs[3 * M + 1]
        part, width = sums[0].shape
        for r in range(M):
            x[:, lanes(f ^ r, width)] = (feats[r][...].astype(F32) + sums[r][...].astype(F32)).astype(BF)
        ahid = dot(x[...], wa[...])
        x[...] = (x[...].astype(F32) + silu(ahid)).astype(BF)
        for r in range(M):
            outs[r][...] = x[:, lanes(f ^ r, width)]

    def gather(info, *refs):
        f = info[0] % M
        parts, ids, sent, ride = refs[:M], refs[M], refs[M + 1], refs[M + 2]
        srcs, tgt, (table, onehot, src) = refs[M + 3 : 2 * M + 3], refs[2 * M + 3], refs[2 * M + 4 :]
        part, width = parts[0].shape
        half = table.shape[0]
        share = ride.shape[1]
        for r in range(M):
            q = f ^ r
            per_half = half // part
            rows = pl.ds(pl.multiple_of(lax.rem(q, per_half) * part, part), part)
            table[rows, lanes(lax.div(q, per_half), width)] = parts[r][...]

        spread = lax.broadcasted_iota(jnp.int32, (CAP, LANES), 1).astype(F32)

        def mark(row, line):
            upper = row >= half
            row = jnp.where(upper, row - half, row)
            lines = [row & (LANES - 1), row >> LANE_BITS, upper.astype(jnp.int32), jnp.zeros((5, CAP), jnp.int32)]
            cols = jnp.transpose(jnp.concatenate(lines, axis=0).astype(F32))
            near = (spread == cols[:, 0:1]).astype(F32).astype(BF)
            far = jnp.broadcast_to(cols[:, 1:2], (CAP, LANES)).astype(BF)
            for h in range(half // LANES):
                onehot[line * CAP : (line + 1) * CAP, h * LANES : (h + 1) * LANES] = jnp.where(
                    far == BF(h), near, jnp.zeros_like(near)
                )
            return cols[:, 2:3] > 0.5

        def pick(line, upper):
            found = dot(onehot[line * CAP : (line + 1) * CAP, :], table[...])
            return jnp.where(upper, found[:, width:], found[:, :width]).astype(BF)

        lines = sent[...].astype(F32)
        n = CAP // LANES
        high = jnp.concatenate([lines[c * G : (c + 1) * G, :] for c in range(n)], axis=1)
        low = jnp.concatenate([lines[(n + c) * G : (n + c + 1) * G, :] for c in range(n)], axis=1)
        src[...] = (high * DIGIT + low).astype(jnp.int32)
        group = onehot.shape[0] // CAP
        places = [(r, s) for r in range(M) for s in range(per)]
        for start in range(0, G, group):
            now = places[start : start + group]
            upper = [mark(src[pl.ds(at(f ^ r, s), 1), :], j) for j, (r, s) in enumerate(now)]
            for j, (r, s) in enumerate(now):
                srcs[r][s * CAP : (s + 1) * CAP, :] = pick(j, upper[j])

        def several(b, _):
            upper = [mark(ids[b * group + j], j) for j in range(group)]
            for j in range(group):
                tgt[b * group + j, :CAP, :] = pick(j, upper[j])
                for k in range(M):
                    tgt[b * group + j, CAP + k * share : CAP + (k + 1) * share, :] = ride[k]
            return 0

        lax.fori_loop(0, G // group, several, 0, unroll=True)

    def edges(info, *refs):
        m = info[1]
        srcs, (shares, tgt, total) = refs[:M], refs[M : M + 3]
        outs, (x, we) = refs[M + 3 : 2 * M + 3], refs[2 * M + 3 :]
        width = srcs[0].shape[1]

        @pl.when(pl.program_id(0) == 0)
        def _():
            put_weights(m, shares, we)

        for r in range(M):
            f = m ^ r
            x[:, lanes(f, width)] = (srcs[r][...].astype(F32) * tgt[0, f].astype(F32)).astype(BF)
        ehid = dot(x[...], we[...])
        x[...] = (total[...] + silu(ehid)).astype(BF)
        for k in range(M):
            outs[k][...] = x[:, lanes(m ^ k, width)]

    def assemble(info, *refs):
        m = info[1]
        parts, out = refs[:M], refs[M]
        for k in range(M):
            for s in range(per):
                out[block_rows(at(m ^ k, s)), :] = parts[k][s * CAP : (s + 1) * CAP, :]

    def assemble_atoms(info, *refs):
        m = info[1]
        parts, out = refs[:M], refs[M]
        part = parts[0].shape[0]
        for r in range(M):
            out[pl.ds(pl.multiple_of((m ^ r) * part, part), part), :] = parts[r][...]

    def local(ef, esrc, etgt, live, partner, mask, basis, af, w_msg, w_down, w_bil, w_up, w_atom, w_edge):
        rows, width = ef.shape
        atoms = af.shape[0]
        depth = w_msg.shape[0]
        dt = w_down.shape[1]
        chunk = per * CAP
        id_rows = ID_ROWS + 2 * rows // LANES
        part = atoms // M
        g = lax.axis_index("graph")
        m = lax.axis_index("mp")
        info = jnp.stack([g, m, jnp.int32(atoms)]).astype(jnp.int32)
        share = depth // G
        first = call(
            split,
            [sds((chunk, width))] * M + [sds((3 * share + dt, width))] + [sds((part, width))] * M,
            jnp.zeros((1,), jnp.int32),
            [ef, w_msg, w_atom, w_edge, w_up, af],
            scratch=[pltpu.SemaphoreType.DMA((M * per + M + 4,))],
            in_specs=[pl.BlockSpec(memory_space=pl.ANY)] * 6,
            vmem=60 * 1024 * 1024,
        )
        chunks, w, feats = first[:M], first[M], first[M + 1 :]
        ws = [w] + [over_mp(w, k) for k in range(1, M)]
        xs = [chunks[0]] + [over_mp(chunks[k], k) for k in range(1, M)]
        wm, wa, we = call(
            stack,
            [sds((M * share, width)), sds((M, share, width)), sds((M, share, width))],
            info,
            ws,
            flops=3e10,
        )
        even = [wm] + [over_plane(wm, x) for x in range(2, G, 2)]
        odd = [over_plane(w, 1) for w in even]
        wm = [w for pair in zip(even, odd) for w in pair]

        blk = lambda i, info: at(info[1], i)
        x, bil = call(
            triplets,
            [sds((chunk, depth)), sds((chunk, dt))],
            info,
            xs + [partner, mask, basis, w_down.T, w_bil.T],
            scratch=[pltpu.VMEM((NB * dt, CAP), BF)],
            grid=(per,),
            in_specs=[pl.BlockSpec((CAP, width), lambda i, info: (i, 0))] * M
            + [pl.BlockSpec((SLOTS, CAP), lambda i, info: (0, blk(i, info)))] * 2
            + [pl.BlockSpec((CAP, SLOTS * NB), lambda i, info: (blk(i, info), 0)), None, None],
            out_specs=[
                pl.BlockSpec((CAP, depth), lambda i, info: (i, 0)),
                pl.BlockSpec((CAP, dt), lambda i, info: (i, 0)),
            ],
        )
        total, outgoing = call(
            messages,
            [sds((chunk, depth), F32), sds((per, M, CAP + id_rows + M // 2 * share, width))],
            info,
            ws + wm + [wa, x, bil, live.reshape(G, CAP), etgt.reshape(G, CAP), esrc.reshape(G, CAP)],
            scratch=[pltpu.VMEM((depth, depth), BF), pltpu.VMEM((dt, depth), BF)],
            grid=(per,),
            in_specs=[None] * (M + G + 1)
            + [
                pl.BlockSpec((CAP, depth), lambda i, info: (i, 0)),
                pl.BlockSpec((CAP, dt), lambda i, info: (i, 0)),
                None,
                None,
                None,
            ],
            out_specs=[
                pl.BlockSpec((CAP, depth), lambda i, info: (i, 0)),
                pl.BlockSpec((1, M, CAP + id_rows + M // 2 * share, width), lambda i, info: (i, 0, 0, 0)),
            ],
        )
        incoming = lax.all_to_all(
            outgoing.reshape(G, CAP + id_rows + M // 2 * share, width), "graph", split_axis=0, concat_axis=0, tiled=True
        )
        feats = [away(feats[r], r) for r in range(M)]
        (token,) = call(
            arrived,
            [sds((8, LANES), F32)],
            info,
            feats,
            in_specs=[pl.BlockSpec(memory_space=pl.ANY)] * M,
            flops=3e10,
        )
        *sums, ids, sent, wa = call(
            aggregate,
            [sds((part, width))] * M + [sds((G, 1, CAP), jnp.int32), sds((2 * rows // LANES, width)), sds((G, M // 2 * share, width))],
            info,
            [incoming, token],
            scratch=[pltpu.VMEM((part, G * CAP), BF), pltpu.VMEM((G * CAP, 2 * width), BF), pltpu.VMEM((atoms, width), BF)],
            flops=3.0e9,
        )
        sums = [sums[0]] + [over_plane(sums[r], r) for r in range(1, M)]
        (wa,) = call(whole_weight, [sds((depth, depth))], info, [wa, over_plane(wa, 1)], flops=1e9)
        outs = call(
            atom_layer,
            [sds((part, width))] * M,
            info,
            sums + feats + [wa],
            scratch=[pltpu.VMEM((part, depth), BF)],
            flops=1.5e9,
        )
        homeward = [home(outs[r], r) for r in range(M)]
        outs = [outs[0]] + [over_plane(outs[r], r) for r in range(1, M)]
        *srcs, named = call(
            gather,
            [sds((chunk, width))] * M + [sds((G, CAP + M * share, width))],
            info,
            outs + [ids, sent, we],
            scratch=[
                pltpu.VMEM((atoms // 2, 2 * width), BF),
                pltpu.VMEM((min(G, 8) * CAP, atoms // 2), BF),
                pltpu.VMEM((G, CAP), jnp.int32),
            ],
            flops=6.0e9,
        )
        srcs = [home(srcs[r], r) for r in range(M)]
        *homeward, named = lax.optimization_barrier((*homeward, named))
        tgt = lax.all_to_all(named, "graph", split_axis=0, concat_axis=0, tiled=True)
        outs = call(
            edges,
            [sds((chunk, width))] * M,
            info,
            srcs + [tgt, tgt.reshape(per, M, CAP + M * share, width), total],
            scratch=[pltpu.VMEM((CAP, depth), BF), pltpu.VMEM((depth, depth), BF)],
            grid=(per,),
            in_specs=[pl.BlockSpec((CAP, width), lambda i, info: (i, 0))] * M
            + [
                pl.BlockSpec((G, M * share, width), lambda i, info: (0, CAP // (M * share), 0)),
                pl.BlockSpec((1, M, CAP, width), lambda i, info: (i, 0, 0, 0)),
                pl.BlockSpec((CAP, depth), lambda i, info: (i, 0)),
            ],
            out_specs=[pl.BlockSpec((CAP, width), lambda i, info: (i, 0))] * M,
        )
        outs = [outs[0]] + [over_mp(outs[k], k) for k in range(1, M)]
        (atom_out,) = call(assemble_atoms, [sds((atoms, width))], info, homeward, flops=1.0e9)
        (edge_out,) = call(assemble, [sds((rows, width))], info, list(outs), flops=1.0e9)
        return (edge_out, atom_out)

    return jax.shard_map(
        local,
        mesh=mesh,
        in_specs=(
            P("graph", "mp"),
            P("graph"),
            P("graph"),
            P("graph"),
            P(None, "graph"),
            P(None, "graph"),
            P("graph", None),
            P("graph", "mp"),
            P(None, "mp"),
            P(),
            P(),
            P(None, "mp"),
            P(None, "mp"),
            P(None, "mp"),
        ),
        out_specs=(P("graph", "mp"), P("graph", "mp")),
        check_vma=False,
    )
```

```python
import functools

import jax
import jax.numpy as jnp
from jax import lax
from jax.experimental import pallas as pl
from jax.experimental.pallas import tpu as pltpu
from jax.sharding import PartitionSpec as P

NB = 16
SLOTS = 8
CAP = 256
LANES = 128
LANE_BITS = 7
DIGIT = 64
DIGIT_BITS = 6
ID_ROWS = 16
BF = jnp.bfloat16
F32 = jnp.float32
VMEM_LIMIT = 40 * 1024 * 1024


def silu(v):
    return v / (1.0 + jnp.exp(-v))


def dot(a, b):
    return jnp.dot(a, b, preferred_element_type=F32)


def dot_t(a, b):
    return lax.dot_general(a, b, (((1,), (1,)), ((), ())), preferred_element_type=F32)


def call(kernel, out_shapes, info, args, scratch=(), grid=(1,), in_specs=None, out_specs=None, flops=0, moved=0, vmem=VMEM_LIMIT):
    whole = lambda s: pl.BlockSpec(s.shape, functools.partial(lambda n, *_: (0,) * n, len(s.shape)))
    in_specs = [whole(a) if in_specs is None or in_specs[i] is None else in_specs[i] for i, a in enumerate(args)]
    out_specs = [
        whole(o) if out_specs is None or out_specs[i] is None else out_specs[i] for i, o in enumerate(out_shapes)
    ]
    return pl.pallas_call(
        kernel,
        out_shape=list(out_shapes),
        grid_spec=pltpu.PrefetchScalarGridSpec(
            num_scalar_prefetch=1, grid=grid, in_specs=in_specs, out_specs=out_specs, scratch_shapes=list(scratch)
        ),
        compiler_params=pltpu.CompilerParams(vmem_limit_bytes=vmem),
        cost_estimate=pl.CostEstimate(flops=int(flops), bytes_accessed=moved, transcendentals=0),
    )(info, *args)


def sds(shape, dtype=BF):
    return jax.ShapeDtypeStruct(tuple(shape), dtype)


def block_rows(i):
    return pl.ds(pl.multiple_of(i * CAP, CAP), CAP)


def lanes(i, width):
    return pl.ds(pl.multiple_of(i * width, width), width)


def column(row):
    wide = jnp.broadcast_to(row.astype(F32), (8, row.shape[1]))
    return jnp.transpose(wide)[:, :1].astype(jnp.int32)


def solution(mesh):
    G = mesh.shape["graph"]
    M = mesh.shape["mp"]
    per = G // M
    both = ("graph", "mp")

    def over_mp(x, k):
        return lax.ppermute(x, "mp", [(i, i ^ k) for i in range(M)])

    def over_plane(x, k):
        return lax.ppermute(x, "graph", [(i, i ^ k) for i in range(G)])

    def at(plane, slot):
        return slot * M + plane

    devices = [(s, i, z) for s in range(per) for i in range(M) for z in range(M)]

    def home(x, r):
        return lax.ppermute(x, both, [(at(i, s) * M + z, at(z, s) * M + (i ^ r)) for s, i, z in devices])

    def away(x, r):
        return lax.ppermute(x, both, [(at(j, s) * M + m, at(m ^ r, s) * M + j) for s, j, m in devices])

    def split(info, ef, wm, wa, we, wu, af, *refs):
        g, m = lax.axis_index("graph"), lax.axis_index("mp")
        outs, share, quarters, sem = refs[:M], refs[M], refs[M + 1 : 2 * M + 1], refs[2 * M + 1]
        part = quarters[0].shape[0]
        moves = []
        for k in range(M):
            for s in range(per):
                moves.append((ef.at[block_rows(at(m ^ k, s)), :], outs[k].at[s * CAP : (s + 1) * CAP, :]))
        start = 0
        for w in (wm, wa, we):
            n = w.shape[0] // G
            moves.append((w.at[pl.ds(pl.multiple_of(g * n, n), n), :], share.at[start : start + n, :]))
            start += n
        moves.append((wu, share.at[start:, :]))
        for r in range(M):
            moves.append((af.at[pl.ds(pl.multiple_of((m ^ r) * part, part), part), :], quarters[r].at[:, :]))
        copies = [pltpu.make_async_copy(src, dst, sem.at[i]) for i, (src, dst) in enumerate(moves)]
        for c in copies:
            c.start()
        for c in copies:
            c.wait()

    def stack(info, *refs):
        parts, (wm, wa, we) = refs[:M], refs[M:]
        n = we.shape[1]
        for k in range(M):
            wm[k * n : (k + 1) * n, :] = parts[k][:n, :]
            wa[k] = parts[k][n : 2 * n, :]
            we[k] = parts[k][2 * n : 3 * n, :]

    def digits(ids):
        return (ids >> DIGIT_BITS).astype(F32), (ids & (DIGIT - 1)).astype(F32)

    def triplets(info, *refs):
        m = info[1]
        xs, (partner, mask, basis, wdt, wbt, x_out, bil_out, mixed) = refs[:M], refs[M:]
        w = xs[0].shape[1]
        for k in range(M):
            x_out[:, lanes(m ^ k, w)] = xs[k][...]
        downt = dot_t(wdt[...], x_out[...]).astype(BF)
        dt = downt.shape[0]
        ids = partner[...] & (CAP - 1)
        rows = lax.broadcasted_iota(jnp.int32, (CAP, CAP), 0)
        picked = []
        for s in range(SLOTS):
            onehot = (rows == ids[s : s + 1, :]).astype(F32).astype(BF)
            picked.append(dot(downt, onehot))
        basist = jnp.transpose(basis[...].astype(F32))
        maskf = mask[...].astype(F32)
        weight = [basist[s * NB : (s + 1) * NB, :] * maskf[s : s + 1, :] for s in range(SLOTS)]
        for b in range(NB):
            acc = weight[0][b : b + 1, :] * picked[0]
            for s in range(1, SLOTS):
                acc = acc + weight[s][b : b + 1, :] * picked[s]
            mixed[b * dt : (b + 1) * dt, :] = acc.astype(BF)
        bilt = dot(wbt[...], mixed[...])
        bil_out[...] = jnp.transpose(bilt).astype(BF)

    def put_weights(m, shares, dst):
        n, width = shares.shape[1] // M, shares.shape[2]

        def put(g, _):
            for k in range(M):
                dst[pl.ds(pl.multiple_of(g * n, n), n), lanes(m ^ k, width)] = shares[g, k * n : (k + 1) * n, :]
            return 0

        lax.fori_loop(0, G, put, 0, unroll=G <= 8)

    def put_shares(info, shares, dst):
        g, m = info[0], info[1]
        n, width = shares[0].shape[0] // M, shares[0].shape[1]
        for d in range(G):
            for k in range(M):
                here = pl.ds(pl.multiple_of((g ^ d) * n, n), n)
                dst[here, lanes(m ^ k, width)] = shares[d][k * n : (k + 1) * n, :]

    def whole_weight(info, own, other, wa):
        g, m = info[0], info[1]
        n, width = own.shape[1] // (M // 2), own.shape[2]

        def put(d, _):
            for core, half in ((g % 2, own), ((g + 1) % 2, other)):
                for j in range(M // 2):
                    cols = lanes(m ^ (core * (M // 2) + j), width)
                    wa[pl.ds(pl.multiple_of(d * n, n), n), cols] = half[d, j * n : (j + 1) * n, :]
            return 0

        lax.fori_loop(0, G, put, 0, unroll=G <= 8)

    def messages(info, *refs):
        m, atoms = info[1], info[2]
        up, shares, (ride, x, bil, live, tgt, src, total_out, out, wm, wu) = refs[:M], refs[M : M + G], refs[M + G :]
        width = out.shape[3]
        dt = wu.shape[0]

        @pl.when(pl.program_id(0) == 0)
        def _():
            put_shares(info, shares, wm)
            for k in range(M):
                wu[:, lanes(m ^ k, width)] = up[k][up[k].shape[0] - dt :, :]

        hid = dot(x[...], wm[...])
        total = x[...].astype(F32) + silu(hid) + dot(bil[...], wu[...])
        total_out[...] = total
        block = pl.ds(at(m, pl.program_id(0)), 1)
        sent = (total * column(live[block, :]).astype(F32)).astype(BF)
        ends = [digits(lax.rem(ids, atoms)) for ids in (tgt[block, :], src[...])]
        lines = [[x[:, c : c + LANES] for x in pair for c in range(0, CAP, LANES)] for pair in ends]
        lines[0].append(jnp.zeros((ID_ROWS - len(lines[0]), LANES), F32))
        lines = [jnp.concatenate(part, axis=0).astype(BF) for part in lines]
        id_rows = CAP + ID_ROWS + lines[1].shape[0]
        for f in range(M):
            out[0, f, :CAP, :] = sent[:, f * width : (f + 1) * width]
            out[0, f, CAP : CAP + ID_ROWS, :] = lines[0]
            out[0, f, CAP + ID_ROWS : id_rows, :] = lines[1]
            for j in range(M // 2):
                here = slice(id_rows + j * ride.shape[1], id_rows + (j + 1) * ride.shape[1])
                out[0, f, here, :] = ride[f % 2 * (M // 2) + j]

    def arrived(info, *refs):
        refs[-1][...] = jnp.zeros(refs[-1].shape, F32)

    def aggregate(info, incoming, _, *refs):
        f = info[0] % M
        outs, (ids, sent, ride, onehot, values, agg) = refs[:M], refs[M:]
        part, width = outs[0].shape
        half = agg.shape[0] // 2
        step = onehot.shape[0]
        low = lax.broadcasted_iota(jnp.int32, (LANES, CAP), 0)

        def place(g, _):
            lines = incoming[g, CAP : CAP + ID_ROWS, :].astype(F32)
            n = CAP // LANES
            high = jnp.concatenate([lines[c : c + 1, :] for c in range(n)], axis=1)
            row = high * DIGIT + jnp.concatenate([lines[n + c : n + c + 1, :] for c in range(n)], axis=1)
            ids[g] = row.astype(jnp.int32)
            ride[g] = incoming[g, incoming.shape[1] - ride.shape[1] :, :]
            upper = (column(row) >= half).astype(F32)
            rows = incoming[g, :CAP, :].astype(F32)
            values[block_rows(g), :width] = (rows * (1.0 - upper)).astype(BF)
            values[block_rows(g), width:] = (rows * upper).astype(BF)
            return 0

        lax.fori_loop(0, G, place, 0, unroll=G <= 8)
        n = CAP + ID_ROWS
        sent[...] = incoming[at(info[1], info[0] // M), n : n + sent.shape[0], :]
        for q in range(half // step):

            def fill(g, _):
                row = ids[g]
                row = jnp.where(row >= half, row - half, row)
                near = (low == (row & (LANES - 1))).astype(F32).astype(BF)
                far = jnp.broadcast_to(((row >> LANE_BITS) - q * (step // LANES)).astype(F32), (LANES, CAP)).astype(BF)
                for h in range(step // LANES):
                    onehot[h * LANES : (h + 1) * LANES, lanes(g, CAP)] = jnp.where(
                        far == BF(h), near, jnp.zeros_like(near)
                    )
                return 0

            lax.fori_loop(0, G, fill, 0, unroll=G <= 8)
            acc = dot(onehot[...], values[...]).astype(BF)
            agg[q * step : (q + 1) * step, :] = acc[:, :width]
            agg[half + q * step : half + (q + 1) * step, :] = acc[:, width:]
        for r in range(M):
            outs[r][...] = agg[pl.ds(pl.multiple_of((f ^ r) * part, part), part), :]

    def atom_layer(info, *refs):
        g, m = info[0], info[1]
        f = g % M
        sums, feats, wa = refs[:M], refs[M : 2 * M], refs[2 * M]
        outs, x = refs[2 * M + 1 : 3 * M + 1], refs[3 * M + 1]
        part, width = sums[0].shape
        for r in range(M):
            x[:, lanes(f ^ r, width)] = (feats[r][...].astype(F32) + sums[r][...].astype(F32)).astype(BF)
        ahid = dot(x[...], wa[...])
        x[...] = (x[...].astype(F32) + silu(ahid)).astype(BF)
        for r in range(M):
            outs[r][...] = x[:, lanes(f ^ r, width)]

    def gather(info, *refs):
        f = info[0] % M
        parts, ids, sent, ride = refs[:M], refs[M], refs[M + 1], refs[M + 2]
        srcs, tgt, (table, onehot, src) = refs[M + 3 : 2 * M + 3], refs[2 * M + 3], refs[2 * M + 4 :]
        part, width = parts[0].shape
        half = table.shape[0]
        share = ride.shape[1]
        for r in range(M):
            q = f ^ r
            per_half = half // part
            rows = pl.ds(pl.multiple_of(lax.rem(q, per_half) * part, part), part)
            table[rows, lanes(lax.div(q, per_half), width)] = parts[r][...]

        spread = lax.broadcasted_iota(jnp.int32, (CAP, LANES), 1).astype(F32)

        def mark(row, line):
            upper = row >= half
            row = jnp.where(upper, row - half, row)
            lines = [row & (LANES - 1), row >> LANE_BITS, upper.astype(jnp.int32), jnp.zeros((5, CAP), jnp.int32)]
            cols = jnp.transpose(jnp.concatenate(lines, axis=0).astype(F32))
            near = (spread == cols[:, 0:1]).astype(F32).astype(BF)
            far = jnp.broadcast_to(cols[:, 1:2], (CAP, LANES)).astype(BF)
            for h in range(half // LANES):
                onehot[line * CAP : (line + 1) * CAP, h * LANES : (h + 1) * LANES] = jnp.where(
                    far == BF(h), near, jnp.zeros_like(near)
                )
            return cols[:, 2:3] > 0.5

        def pick(found, line, upper):
            found = found[line * CAP : (line + 1) * CAP, :]
            return jnp.where(upper, found[:, width:], found[:, :width]).astype(BF)

        lines = sent[...].astype(F32)
        n = CAP // LANES
        high = jnp.concatenate([lines[c * G : (c + 1) * G, :] for c in range(n)], axis=1)
        low = jnp.concatenate([lines[(n + c) * G : (n + c + 1) * G, :] for c in range(n)], axis=1)
        src[...] = (high * DIGIT + low).astype(jnp.int32)
        group = onehot.shape[0] // CAP
        places = [(r, s) for r in range(M) for s in range(per)]
        for start in range(0, G, group):
            now = places[start : start + group]
            upper = [mark(src[pl.ds(at(f ^ r, s), 1), :], j) for j, (r, s) in enumerate(now)]
            found = dot(onehot[...], table[...])
            for j, (r, s) in enumerate(now):
                srcs[r][s * CAP : (s + 1) * CAP, :] = pick(found, j, upper[j])

        def several(b, _):
            upper = [mark(ids[b * group + j], j) for j in range(group)]
            found = dot(onehot[...], table[...])
            for j in range(group):
                tgt[b * group + j, :CAP, :] = pick(found, j, upper[j])
                for k in range(M):
                    tgt[b * group + j, CAP + k * share : CAP + (k + 1) * share, :] = ride[k]
            return 0

        lax.fori_loop(0, G // group, several, 0, unroll=True)

    def edges(info, *refs):
        m = info[1]
        srcs, (shares, tgt, total) = refs[:M], refs[M : M + 3]
        outs, (x, we) = refs[M + 3 : 2 * M + 3], refs[2 * M + 3 :]
        width = srcs[0].shape[1]

        @pl.when(pl.program_id(0) == 0)
        def _():
            put_weights(m, shares, we)

        for r in range(M):
            f = m ^ r
            x[:, lanes(f, width)] = (srcs[r][...].astype(F32) * tgt[0, f].astype(F32)).astype(BF)
        ehid = dot(x[...], we[...])
        x[...] = (total[...] + silu(ehid)).astype(BF)
        for k in range(M):
            outs[k][...] = x[:, lanes(m ^ k, width)]

    def assemble(info, *refs):
        m = info[1]
        parts, out = refs[:M], refs[M]
        for k in range(M):
            for s in range(per):
                out[block_rows(at(m ^ k, s)), :] = parts[k][s * CAP : (s + 1) * CAP, :]

    def assemble_atoms(info, *refs):
        m = info[1]
        parts, out = refs[:M], refs[M]
        part = parts[0].shape[0]
        for r in range(M):
            out[pl.ds(pl.multiple_of((m ^ r) * part, part), part), :] = parts[r][...]

    def local(ef, esrc, etgt, live, partner, mask, basis, af, w_msg, w_down, w_bil, w_up, w_atom, w_edge):
        rows, width = ef.shape
        atoms = af.shape[0]
        depth = w_msg.shape[0]
        dt = w_down.shape[1]
        chunk = per * CAP
        id_rows = ID_ROWS + 2 * rows // LANES
        part = atoms // M
        g = lax.axis_index("graph")
        m = lax.axis_index("mp")
        info = jnp.stack([g, m, jnp.int32(atoms)]).astype(jnp.int32)
        share = depth // G
        first = call(
            split,
            [sds((chunk, width))] * M + [sds((3 * share + dt, width))] + [sds((part, width))] * M,
            jnp.zeros((1,), jnp.int32),
            [ef, w_msg, w_atom, w_edge, w_up, af],
            scratch=[pltpu.SemaphoreType.DMA((M * per + M + 4,))],
            in_specs=[pl.BlockSpec(memory_space=pl.ANY)] * 6,
            vmem=60 * 1024 * 1024,
        )
        chunks, w, feats = first[:M], first[M], first[M + 1 :]
        ws = [w] + [over_mp(w, k) for k in range(1, M)]
        xs = [chunks[0]] + [over_mp(chunks[k], k) for k in range(1, M)]
        wm, wa, we = call(
            stack,
            [sds((M * share, width)), sds((M, share, width)), sds((M, share, width))],
            info,
            ws,
            flops=3e10,
        )
        even = [wm] + [over_plane(wm, x) for x in range(2, G, 2)]
        odd = [over_plane(w, 1) for w in even]
        wm = [w for pair in zip(even, odd) for w in pair]

        blk = lambda i, info: at(info[1], i)
        x, bil = call(
            triplets,
            [sds((chunk, depth)), sds((chunk, dt))],
            info,
            xs + [partner, mask, basis, w_down.T, w_bil.T],
            scratch=[pltpu.VMEM((NB * dt, CAP), BF)],
            grid=(per,),
            in_specs=[pl.BlockSpec((CAP, width), lambda i, info: (i, 0))] * M
            + [pl.BlockSpec((SLOTS, CAP), lambda i, info: (0, blk(i, info)))] * 2
            + [pl.BlockSpec((CAP, SLOTS * NB), lambda i, info: (blk(i, info), 0)), None, None],
            out_specs=[
                pl.BlockSpec((CAP, depth), lambda i, info: (i, 0)),
                pl.BlockSpec((CAP, dt), lambda i, info: (i, 0)),
            ],
        )
        total, outgoing = call(
            messages,
            [sds((chunk, depth), F32), sds((per, M, CAP + id_rows + M // 2 * share, width))],
            info,
            ws + wm + [wa, x, bil, live.reshape(G, CAP), etgt.reshape(G, CAP), esrc.reshape(G, CAP)],
            scratch=[pltpu.VMEM((depth, depth), BF), pltpu.VMEM((dt, depth), BF)],
            grid=(per,),
            in_specs=[None] * (M + G + 1)
            + [
                pl.BlockSpec((CAP, depth), lambda i, info: (i, 0)),
                pl.BlockSpec((CAP, dt), lambda i, info: (i, 0)),
                None,
                None,
                None,
            ],
            out_specs=[
                pl.BlockSpec((CAP, depth), lambda i, info: (i, 0)),
                pl.BlockSpec((1, M, CAP + id_rows + M // 2 * share, width), lambda i, info: (i, 0, 0, 0)),
            ],
        )
        incoming = lax.all_to_all(
            outgoing.reshape(G, CAP + id_rows + M // 2 * share, width), "graph", split_axis=0, concat_axis=0, tiled=True
        )
        feats = [away(feats[r], r) for r in range(M)]
        (token,) = call(
            arrived,
            [sds((8, LANES), F32)],
            info,
            feats,
            in_specs=[pl.BlockSpec(memory_space=pl.ANY)] * M,
            flops=3e10,
        )
        *sums, ids, sent, wa = call(
            aggregate,
            [sds((part, width))] * M + [sds((G, 1, CAP), jnp.int32), sds((2 * rows // LANES, width)), sds((G, M // 2 * share, width))],
            info,
            [incoming, token],
            scratch=[pltpu.VMEM((part, G * CAP), BF), pltpu.VMEM((G * CAP, 2 * width), BF), pltpu.VMEM((atoms, width), BF)],
            flops=3.0e9,
        )
        sums = [sums[0]] + [over_plane(sums[r], r) for r in range(1, M)]
        (wa,) = call(whole_weight, [sds((depth, depth))], info, [wa, over_plane(wa, 1)], flops=1e9)
        outs = call(
            atom_layer,
            [sds((part, width))] * M,
            info,
            sums + feats + [wa],
            scratch=[pltpu.VMEM((part, depth), BF)],
            flops=1.5e9,
        )
        homeward = [home(outs[r], r) for r in range(M)]
        outs = [outs[0]] + [over_plane(outs[r], r) for r in range(1, M)]
        *srcs, named = call(
            gather,
            [sds((chunk, width))] * M + [sds((G, CAP + M * share, width))],
            info,
            outs + [ids, sent, we],
            scratch=[
                pltpu.VMEM((atoms // 2, 2 * width), BF),
                pltpu.VMEM((min(G, 8) * CAP, atoms // 2), BF),
                pltpu.VMEM((G, CAP), jnp.int32),
            ],
            flops=6.0e9,
        )
        srcs = [home(srcs[r], r) for r in range(M)]
        *homeward, named = lax.optimization_barrier((*homeward, named))
        tgt = lax.all_to_all(named, "graph", split_axis=0, concat_axis=0, tiled=True)
        outs = call(
            edges,
            [sds((chunk, width))] * M,
            info,
            srcs + [tgt, tgt.reshape(per, M, CAP + M * share, width), total],
            scratch=[pltpu.VMEM((CAP, depth), BF), pltpu.VMEM((depth, depth), BF)],
            grid=(per,),
            in_specs=[pl.BlockSpec((CAP, width), lambda i, info: (i, 0))] * M
            + [
                pl.BlockSpec((G, M * share, width), lambda i, info: (0, CAP // (M * share), 0)),
                pl.BlockSpec((1, M, CAP, width), lambda i, info: (i, 0, 0, 0)),
                pl.BlockSpec((CAP, depth), lambda i, info: (i, 0)),
            ],
            out_specs=[pl.BlockSpec((CAP, width), lambda i, info: (i, 0))] * M,
        )
        outs = [outs[0]] + [over_mp(outs[k], k) for k in range(1, M)]
        (atom_out,) = call(assemble_atoms, [sds((atoms, width))], info, homeward, flops=1.0e9)
        (edge_out,) = call(assemble, [sds((rows, width))], info, list(outs), flops=1.0e9)
        return (edge_out, atom_out)

    return jax.shard_map(
        local,
        mesh=mesh,
        in_specs=(
            P("graph", "mp"),
            P("graph"),
            P("graph"),
            P("graph"),
            P(None, "graph"),
            P(None, "graph"),
            P("graph", None),
            P("graph", "mp"),
            P(None, "mp"),
            P(),
            P(),
            P(None, "mp"),
            P(None, "mp"),
            P(None, "mp"),
        ),
        out_specs=(P("graph", "mp"), P("graph", "mp")),
        check_vma=False,
    )
```
